32 devices in a mesh: groups: 2 (over y), fluid: 4 (over z), metal: 2 (over x), span: 2 (over core).
Axes of the slice: x: 2, y: 2, z: 4, core: 2. Of those that a mesh axis runs over, the one named last changes fastest.
Arguments:
- fluid_temp: bfloat16 [64, 8, 128, 512], P(('groups', 'fluid', 'metal'), None, None, 'span'), parts along dimension 0, may hold values from -6 to 6
- wall_old: float32 [64, 128, 512], P(('groups', 'fluid', 'metal'), None, 'span'), parts along dimension 0, may hold values from -6 to 6
- conductance: float32 [64, 128], P(('groups', 'fluid', 'metal')), parts along dimension 0, may hold values from 0.5 to 4
- valid_rows: int32 [64], P(('groups', 'fluid', 'metal')), parts along dimension 0, may hold values from 64 to 128
- face_owner: int32 [64, 128, 1], P(('groups', 'fluid', 'metal')), parts along dimension 0, may hold values from 0 to 3; in each aligned block of 512 rows (0 to 511, 512 to 1023, ..., all dimensions but the last counted through in order) at most 192 rows name the same one
- face_slot: int32 [64, 128], P(('groups', 'fluid', 'metal')), parts along dimension 0, may hold values from 0 to 511
- response: bfloat16 [4, 1024, 1024], P('fluid', 'metal'), as said below
- coolant: float32 [4, 1024], P('fluid', 'metal'), may hold values from 0.5 to 1.5
- flux_old: float32 [8, 1024, 512], P(('groups', 'fluid'), 'metal', 'span'), parts along dimension 0, may hold values from -6 to 6
Outputs:
- flux_avg: float32 [8, 1024, 512], P(('groups', 'fluid'), 'metal', 'span'), parts along dimension 0
- metal_wall: float32 [8, 1024, 512], P(('groups', 'fluid'), 'metal', 'span'), parts along dimension 0
- wall_new: float32 [64, 128, 512], P(('groups', 'fluid', 'metal'), None, 'span'), parts along dimension 0
The draws below stay inside these ranges and needn't reach their ends.
There are 2 independent parts, one for each index of `groups`. The reference program is written for one: setup_inputs(seed, part) draws one part's arguments, and reference() takes and returns one part's arrays. A program takes and returns all parts, laid end to end along the dimension named above; an argument that names none is the same for every part. Nothing has to cross between parts.
Inputs may be any that keep to these rules, and one draw needn't show every extreme that they name: `face_owner`: among the 512 cells of one device's blocks (padded ones included) at most 192 name one owner, and in some device's cells some owner is named exactly 192 times. response[o] is symmetric: response[o, i, j] = response[o, j, i].
All inputs are finite; a program needn't handle non-finite values.
Results may differ from the reference program's by a relative error of at most 0.0017.
Values may be sent and summed in bfloat16 or wider, within the bound.
A program may use at most 64 MiB of HBM per device.

```python
import math
import jax
import jax.numpy as jnp
import numpy as np
from jax import lax

CELLS = 128
LAY = 8
FBD = 4
WSLOT = 512
SPAN = 512
WALL = 1024
OWNERS = 4
FB = 32
CAP = 192
N_FLUID = 4
N_METAL = 2


def draw_response(key, part):
    key = jax.random.fold_in(key, 11)
    first, second = jax.random.split(key)
    raw = jax.random.normal(first, (OWNERS, WALL, WALL), jnp.float32)
    off_diagonal = 0.35 * (raw + jnp.swapaxes(raw, 1, 2)) / math.sqrt(WALL)
    diagonal = jax.random.uniform(second, (OWNERS, WALL), jnp.float32, 0.6, 1.4)
    identity = jnp.arange(WALL)[:, None] == jnp.arange(WALL)[None, :]
    return jnp.where(identity[None], diagonal[:, :, None], off_diagonal).astype(jnp.bfloat16)


def set_ends(values, key, low, top_value):
    shape = values.shape
    place = [jax.random.randint(jax.random.fold_in(key, axis), (), 0, shape[axis]) for axis in range(len(shape))]
    values = values.at[tuple(place)].set(low)
    longest = shape.index(max(shape))
    place[longest] = (place[longest] + 1) % shape[longest]
    return values.at[tuple(place)].set(top_value)


def levels(key, dims, cuts, least, largest):
    def one(dim, shards_of):
        draws = jax.random.uniform(jax.random.fold_in(jax.random.fold_in(key, 6), dim), (shards_of,), jnp.float32, least / len(cuts), largest / len(cuts))
        return jnp.repeat(jnp.exp(draws), dims[dim] // shards_of).reshape((-1,) + (1,) * (len(dims) - dim - 1))

    level = one(*cuts[0])
    for cut in cuts[1:]:
        level = level * one(*cut)
    return level


def assign_block(rng, own, number, rows, count, top, bound, slope):
    ranking = jax.random.permutation(rng, count)
    packed, usual = shares(count, rows * top, bound, slope, True), shares(count, rows * top, bound, slope, False)
    places = jnp.arange(count)

    def named(sizes, turn):
        used = int((sizes > 0).sum())
        fixed = max(1, used // 4)
        shifted = fixed + (places - fixed + turn * (used - fixed)) % max(1, count - fixed)
        return jnp.zeros((count,), jnp.int32).at[ranking[jnp.where(places < fixed, places, shifted)]].set(jnp.asarray(sizes, jnp.int32))

    sizes = jnp.where(number % 4 == 0, named(packed, number // 4), named(usual, number - number // 4 - 1))
    mixed = jax.random.permutation(jax.random.fold_in(own, 3), count)
    source_of, sink = mixed[0:count // 2 * 2:2], mixed[1:count // 2 * 2:2]
    margin = jnp.minimum(sizes[source_of] - 1, bound - sizes[sink]) // 2
    margin = jnp.where((source_of == ranking[0]) | (sink == ranking[0]) | (sizes[sink] == 0), 0, jnp.maximum(margin, 0))
    shifted = jax.random.randint(jax.random.fold_in(own, 4), (count // 2,), 0, 1 << 20) % (margin + 1)
    sizes = sizes.at[source_of].add(-shifted).at[sink].add(shifted)
    labels = jnp.searchsorted(jnp.cumsum(sizes), jnp.arange(rows * top), side="right").astype(jnp.int32)
    grid = labels.reshape(top, rows).T
    grid = grid[jax.random.permutation(jax.random.fold_in(own, 1), rows)]
    turn = jax.random.randint(jax.random.fold_in(own, 2), (rows, 1), 0, top)
    return jnp.take_along_axis(grid, (jnp.arange(top)[None, :] + turn) % top, axis=1)


def shares(count, total, reach, skew, full):
    loads = [(1 << 20) // math.isqrt(grade ** skew) + 1 for grade in range(1, count + 1)]
    largest = reach if full else min(reach, max(-(-total // count), total * loads[0] // sum(loads)))
    least = 1 if total - largest >= count - 1 else 0
    holding, spare = [largest] + [least] * (count - 1), total - largest - least * (count - 1)
    while spare > 0:
        free = [i for i in range(1, count) if holding[i] < largest] or [i for i in range(1, count) if holding[i] < reach]
        pool, budget = sum([loads[i] for i in free]), spare
        for i in free:
            more = min(reach - holding[i], max(1, budget * loads[i] // pool), spare)
            holding[i] = holding[i] + more
            spare = spare - more
    return np.array(holding)


def centred(rng, extent, spread, limit, shards=(), held_as=jnp.bfloat16):
    level = levels(rng, extent, shards, -0.22, 0.18) if shards else 1.0
    array = jax.random.normal(rng, extent, jnp.float32) * spread * level
    return jnp.minimum(jnp.maximum(array, -limit), limit).astype(held_as)


def setup_inputs(seed: int = 0, part: int = 0) -> dict:
    arg_keys = jax.random.split(jax.random.key(seed), 10)
    own_keys = jax.random.split(jax.random.fold_in(arg_keys[9], part), 10)
    fluid_temp = centred(own_keys[0], (FB, LAY, CELLS, SPAN), 1.0, 6.0, ((0, 8), (3, 2)))
    wall_old = centred(own_keys[1], (FB, CELLS, SPAN), 1.0, 6.0, ((0, 8), (2, 2)), jnp.float32)
    conductance = jnp.clip(jnp.exp(math.log(4.0) - 2.0794415 * jax.random.uniform(own_keys[2], (FB, CELLS), jnp.float32) ** levels(own_keys[2], (FB, CELLS), ((0, 8),), -0.2, 0.2)), 0.5, 4.0)
    valid_rows = set_ends(jax.random.randint(own_keys[3], (FB,), CELLS // 2, CELLS + 1), jax.random.fold_in(own_keys[3], 1), CELLS // 2, CELLS).astype(jnp.int32)
    face_owner_keys = jax.random.split(jax.random.fold_in(own_keys[4], 1), FB * CELLS // (FBD * CELLS))
    face_owner_turns = jax.random.permutation(jax.random.fold_in(own_keys[4], 3), FB * CELLS // (FBD * CELLS))
    face_owner = jax.vmap(lambda own, number: assign_block(jax.random.fold_in(own_keys[4], 2), own, number, FBD * CELLS, N_FLUID, 1, CAP, 2))(face_owner_keys, face_owner_turns).reshape((FB, CELLS, 1))
    face_slot = set_ends(jax.random.randint(own_keys[5], (FB, CELLS), 0, WSLOT), jax.random.fold_in(own_keys[5], 1), 0, WSLOT - 1).astype(jnp.int32)
    response = draw_response(jax.random.fold_in(arg_keys[9], 71), part)
    coolant = jnp.clip(0.5 + 1.0 * jax.random.uniform(arg_keys[7], (OWNERS, WALL), jnp.float32) ** levels(arg_keys[7], (OWNERS, WALL), ((0, 4), (1, 2)), -0.2, 0.2), 0.5, 1.5)
    flux_old = centred(own_keys[8], (OWNERS, WALL, SPAN), 1.0, 6.0, ((0, 4), (1, 2), (2, 2)), jnp.float32)
    return {"fluid_temp": fluid_temp, "wall_old": wall_old, "conductance": conductance, "valid_rows": valid_rows, "face_owner": face_owner, "face_slot": face_slot, "response": response, "coolant": coolant, "flux_old": flux_old}


average_weight = 0.3
span_mix = 0.25
relaxation = 0.5


def apply_owner(operands):
    return jnp.dot(operands[0], operands[1], preferred_element_type=jnp.float32)


def reference(fluid_temp, wall_old, conductance, valid_rows, face_owner, face_slot, response, coolant, flux_old):
    level = jnp.arange(LAY, dtype=jnp.float32)
    weights = 2.0 * (LAY - level) / (LAY * (LAY + 1.0))
    near_wall = jnp.sum(fluid_temp.astype(jnp.float32) * weights[None, :, None, None], axis=1)
    active = jnp.arange(CELLS, dtype=jnp.int32)[None, :] < valid_rows[:, None]
    heat_flux = jnp.where(active[:, :, None], conductance[:, :, None] * (near_wall - wall_old), 0.0)
    column = (jnp.arange(FB, dtype=jnp.int32) // FBD) % N_METAL
    target = face_owner[:, :, 0] * WALL + column[:, None] * WSLOT + face_slot
    target = jnp.where(active, target, OWNERS * WALL).astype(jnp.int32).reshape(-1)
    summed = jnp.zeros((OWNERS * WALL + 1, SPAN), jnp.float32).at[target].add(heat_flux.reshape(-1, SPAN))
    summed = summed[:OWNERS * WALL].reshape(OWNERS, WALL, SPAN)
    flux_avg = (1.0 - average_weight) * flux_old + average_weight * summed
    flux_low = flux_avg.astype(jnp.bfloat16)
    temp_rise = lax.map(apply_owner, (response, flux_low))
    slot_temp = coolant[:, :, None] + temp_rise
    metal_wall = slot_temp + span_mix * (jnp.roll(slot_temp, -1, axis=2) - 2.0 * slot_temp + jnp.roll(slot_temp, 1, axis=2))
    extended = jnp.concatenate([metal_wall.reshape(OWNERS * WALL, SPAN), jnp.zeros((1, SPAN), jnp.float32)], axis=0)
    face_temp = extended[target].reshape(FB, CELLS, SPAN)
    wall_new = jnp.where(active[:, :, None], (1.0 - relaxation) * wall_old + relaxation * face_temp, 0.0)
    return flux_avg, metal_wall, wall_new
```

```python
import functools

import jax
import jax.numpy as jnp
from jax import lax
from jax.experimental import pallas as pl
from jax.experimental.pallas import tpu as pltpu
from jax.sharding import PartitionSpec as P

average_weight = 0.3
span_mix = 0.25
relaxation = 0.5
code_limit = 32512.0
MESH = pl.DeviceIdType.MESH
f32, bf16, i32, i16 = jnp.float32, jnp.bfloat16, jnp.int32, jnp.int16


def mm(a, b):
    return jnp.dot(a, b, preferred_element_type=f32)


def to_column(row):
    eye = lax.broadcasted_iota(i32, (128, 128), 0) == lax.broadcasted_iota(i32, (128, 128), 1)
    return jnp.concatenate(
        [
            jnp.sum(jnp.where(eye, row[:, i : i + 128], 0.0), axis=1, keepdims=True)
            for i in range(0, row.shape[1], 128)
        ],
        axis=0,
    )


def encode(x):
    top = jnp.maximum(jnp.max(jnp.abs(x), keepdims=True), 1e-30)
    code = jnp.floor(x * (code_limit / top) + 0.5)
    return code, top * (1.0 / code_limit)


def code_parts(code):
    high = jnp.floor(code * (1.0 / 256.0) + 0.5)
    return jnp.concatenate([high, code - 256.0 * high], axis=1).astype(bf16)


def from_parts(both):
    half = both.shape[1] // 2
    return 256.0 * both[:, :half] + both[:, half:]


def value_parts(x):
    high = x.astype(bf16)
    return jnp.concatenate([high, (x - high.astype(f32)).astype(bf16)], axis=1)


def add_parts(both):
    half = both.shape[1] // 2
    return both[:, :half] + both[:, half:]


def pick(x, chunk):
    n = x.shape[1]
    if chunk == 0:
        return jnp.concatenate([x[:, 3 * n // 4 :], x[:, : n // 4]], axis=1)
    return x[:, n // 4 : 3 * n // 4]


def unpick(edge, middle):
    half = edge.shape[1] // 2
    return jnp.concatenate([edge[:, half:], middle, edge[:, :half]], axis=1)


def smooth(edge, middle, other):
    width = edge.shape[1]
    x = jnp.concatenate([edge, middle], axis=1)
    low = pltpu.roll(x, 1, 1)
    high = pltpu.roll(x, 2 * width - 1, 1)
    lane = lax.broadcasted_iota(i32, edge.shape, 1)
    low_edge = jnp.where(lane == width // 2, pltpu.roll(other, 1, 1), low[:, :width])
    high_edge = jnp.where(lane == width // 2 - 1, pltpu.roll(other, width - 1, 1), high[:, :width])
    new_edge = edge + span_mix * (high_edge - 2.0 * edge + low_edge)
    new_middle = middle + span_mix * (high[:, width:] - 2.0 * middle + low[:, width:])
    return unpick(new_edge, new_middle)


def kernel(
    fluids, metals, cap,
    valid, fluid_in, wall_in, cond, owner, slot, resp_in, cool, old_in,
    favg_out, mwall_out, wnew_out,
    fluid_v, wall_v, resp_v, old_v,
    pack, unpack, spread, fetch,
    meta_s, meta_r, flux_s, flux_r, fstep_s, fstep_r,
    low_v, temp_v, halo_t, back_s, back_r, bstep_s, bstep_r, face_v, halo_f,
    favg_v, mwall_v, wnew_v,
    local_sem, meta_sem, flux_sem, fstep_sem, low_sem, halo_sem, back_sem, bstep_sem,
):
    blocks, layers, cells, span_dev = fluid_v.shape
    rows = blocks * cells
    slots = resp_v.shape[0]
    width = span_dev // 2
    me_f, me_m, me_s = lax.axis_index("fluid"), lax.axis_index("metal"), lax.axis_index("span")
    up = [None] + [lax.rem(me_f + r, fluids) for r in range(1, fluids)]
    down = [None] + [lax.rem(me_f + fluids - r, fluids) for r in range(1, fluids)]
    across = [None] + [lax.rem(me_m + r, metals) for r in range(1, metals)]
    mate = 1 - me_s

    loads = [
        pltpu.make_async_copy(src, dst, local_sem.at[i])
        for i, (src, dst) in enumerate(
            ((fluid_in, fluid_v), (wall_in, wall_v), (old_in, old_v), (resp_in, resp_v))
        )
    ]
    for load in loads:
        load.start()

    barrier = pltpu.get_barrier_semaphore()
    for r in range(1, fluids):
        pl.semaphore_signal(barrier, inc=1, device_id={"fluid": up[r]}, device_id_type=MESH)
    for r in range(1, metals):
        pl.semaphore_signal(barrier, inc=1, device_id={"metal": across[r]}, device_id_type=MESH)
    pl.semaphore_signal(barrier, inc=1, device_id={"span": mate}, device_id_type=MESH)

    def remote(src, dst, sems, place, where):
        return pltpu.make_async_remote_copy(
            src_ref=src, dst_ref=dst, send_sem=sems.at[(0, *place)], recv_sem=sems.at[(1, *place)],
            device_id=where, device_id_type=MESH,
        )

    away = jnp.concatenate([owner[b : b + 1, :] for b in range(blocks)], axis=1) - me_f
    away = jnp.where(away < 0, away + fluids, away)
    cell = lax.broadcasted_iota(i32, (1, cells), 1)
    live = jnp.concatenate([(cell < valid[b]).astype(i32) for b in range(blocks)], axis=1)
    away = jnp.where(live > 0, away, -1)
    lines = -(-fluids // 16) * 16
    chosen = lax.broadcasted_iota(i32, (lines, rows), 0) == away
    before = lax.broadcasted_iota(i32, (rows, rows), 0) < lax.broadcasted_iota(i32, (rows, rows), 1)
    earlier = mm(chosen.astype(f32).astype(bf16), before.astype(f32).astype(bf16))
    ordinal = jnp.sum(jnp.where(chosen, earlier, 0.0), axis=0, keepdims=True)
    place = jnp.where(away >= 0, away.astype(f32) * cap + ordinal, -1.0)
    total = fluids * cap
    pack[...] = (
        lax.broadcasted_iota(i32, (total, rows), 0).astype(f32) == place
    ).astype(f32).astype(bf16)
    place_col = to_column(place)
    unpack[...] = (
        lax.broadcasted_iota(i32, (rows, total), 1).astype(f32) == place_col
    ).astype(f32).astype(bf16)
    slot_row = jnp.concatenate([slot[b : b + 1, :] for b in range(blocks)], axis=1)
    line = lax.broadcasted_iota(i32, (16, rows), 0)
    halves = jnp.where(line == 0, slot_row // 256, jnp.where(line == 1, slot_row % 256, 0))
    packed_slots = mm(halves.astype(f32).astype(bf16), unpack[...])
    packed_slots = 256.0 * packed_slots[0:1] + packed_slots[1:2]
    for r in range(fluids):
        meta_s[r, :, 0:cap] = jnp.broadcast_to(packed_slots[:, r * cap : (r + 1) * cap], (8, cap))

    pl.semaphore_wait(barrier, fluids + metals - 1)
    sends = []

    def send(copy):
        copy.start()
        sends.append(copy)
        return copy

    metas = [
        send(remote(meta_s.at[r], meta_r.at[r], meta_sem, (r,), {"fluid": up[r]}))
        for r in range(1, fluids)
    ]

    loads[0].wait()
    loads[1].wait()
    weights = [2.0 * (layers - l) / (layers * (layers + 1.0)) for l in range(layers)]
    flux = []
    for b in range(blocks):
        near = weights[0] * fluid_v[b, 0].astype(f32)
        for l in range(1, layers):
            near = near + weights[l] * fluid_v[b, l].astype(f32)
        gain = to_column(cond[b : b + 1, :])
        lives = lax.broadcasted_iota(i32, (cells, 1), 0) < valid[b]
        flux.append(
            jnp.where(lives, gain * (near - wall_v[b * cells : (b + 1) * cells, :]), 0.0)
        )
    flux = jnp.concatenate(flux, axis=0)

    fluxes, fsteps = [], []
    for c in range(2):
        code, step = encode(pick(flux, c))
        fstep_s[c] = jnp.broadcast_to(step, (8, 128))
        packed = from_parts(mm(pack[...], code_parts(code))).astype(i32).astype(i16)
        for r in range(fluids):
            dst = flux_r if r == 0 else flux_s
            dst[c, r] = packed[r * cap : (r + 1) * cap]
        fsteps.append(
            [
                send(remote(fstep_s.at[c], fstep_r.at[c, r], fstep_sem, (c, r), {"fluid": up[r]}))
                for r in range(1, fluids)
            ]
        )
        fluxes.append(
            [
                send(remote(flux_s.at[c, r], flux_r.at[c, r], flux_sem, (c, r), {"fluid": up[r]}))
                for r in range(1, fluids)
            ]
        )

    for copy in metas:
        copy.wait_recv()
    arrived = jnp.concatenate(
        [packed_slots[:, 0:cap]] + [meta_r[r, 0:1, 0:cap] for r in range(1, fluids)], axis=1
    )
    spread[...] = (
        lax.broadcasted_iota(i32, (slots, total), 0).astype(f32) == arrived
    ).astype(f32).astype(bf16)
    fetch[...] = (
        lax.broadcasted_iota(i32, (total, slots), 1).astype(f32) == to_column(arrived)
    ).astype(f32).astype(bf16)
    cool_col = to_column(cool[...])
    loads[2].wait()
    loads[3].wait()

    averages, backs, bsteps = [], [], []
    for c in range(2):
        for copy in fsteps[c] + fluxes[c]:
            copy.wait_recv()
        incoming = jnp.concatenate(
            [
                flux_r[c, r].astype(i32).astype(f32)
                * (fstep_s[c, 0:1, :] if r == 0 else fstep_r[c, r, 0:1, :])
                for r in range(fluids)
            ],
            axis=0,
        )
        summed = add_parts(mm(spread[...], value_parts(incoming)))
        average = (1.0 - average_weight) * pick(old_v[...], c) + average_weight * summed
        averages.append(average)
        low_v[c, 0] = average.astype(bf16)
        lows = [
            send(remote(low_v.at[c, 0], low_v.at[c, r], low_sem, (c, r), {"metal": across[r]}))
            for r in range(1, metals)
        ]
        if c == 1:
            favg_v[...] = unpick(*averages)
            store_favg = pltpu.make_async_copy(favg_v, favg_out, local_sem.at[4])
            store_favg.start()
        temp = cool_col
        for r in range(metals):
            if r:
                lows[r - 1].wait_recv()
            stripe = lax.rem(me_m + metals - r, metals)
            columns = pl.ds(pl.multiple_of(stripe * slots, slots), slots)
            temp = temp + mm(resp_v[:, columns], low_v[c, r])
        temp_v[c] = temp
        if c == 0:
            edge_t = send(remote(temp_v.at[0], halo_t, halo_sem, (0,), {"span": mate}))
        code, step = encode(temp)
        bstep_s[c] = jnp.broadcast_to(step, (8, 128))
        found = from_parts(mm(fetch[...], code_parts(code))).astype(i32).astype(i16)
        for r in range(fluids):
            dst = back_r if r == 0 else back_s
            dst[c, r] = found[r * cap : (r + 1) * cap]
        bsteps.append(
            [
                send(remote(bstep_s.at[c], bstep_r.at[c, r], bstep_sem, (c, r), {"fluid": down[r]}))
                for r in range(1, fluids)
            ]
        )
        backs.append(
            [
                send(remote(back_s.at[c, r], back_r.at[c, r], back_sem, (c, r), {"fluid": down[r]}))
                for r in range(1, fluids)
            ]
        )

    edge_t.wait_recv()
    mwall_v[...] = smooth(temp_v[0], temp_v[1], halo_t[...])
    store_mwall = pltpu.make_async_copy(mwall_v, mwall_out, local_sem.at[5])
    store_mwall.start()

    for c in range(2):
        for copy in bsteps[c] + backs[c]:
            copy.wait_recv()
        returned = jnp.concatenate(
            [
                back_r[c, r].astype(i32).astype(f32)
                * (bstep_s[c, 0:1, :] if r == 0 else bstep_r[c, r, 0:1, :])
                for r in range(fluids)
            ],
            axis=0,
        )
        face_v[c] = add_parts(mm(unpack[...], value_parts(returned)))
        if c == 0:
            edge_f = send(remote(face_v.at[0], halo_f, halo_sem, (1,), {"span": mate}))
    edge_f.wait_recv()
    face = smooth(face_v[0], face_v[1], halo_f[...])
    for b in range(blocks):
        lives = lax.broadcasted_iota(i32, (cells, 1), 0) < valid[b]
        part = slice(b * cells, (b + 1) * cells)
        wnew_v[part, :] = jnp.where(
            lives, (1.0 - relaxation) * wall_v[part, :] + relaxation * face[part], 0.0
        )
    store_wnew = pltpu.make_async_copy(wnew_v, wnew_out, local_sem.at[6])
    store_wnew.start()
    for copy in sends:
        copy.wait_send()
    store_favg.wait()
    store_mwall.wait()
    store_wnew.wait()


def body(
    fluid_temp, wall_old, conductance, valid_rows, face_owner, face_slot, response, coolant, flux_old
):
    blocks, layers, cells, span_dev = fluid_temp.shape
    rows = blocks * cells
    fluids, metals = lax.axis_size("fluid"), lax.axis_size("metal")
    cap = -(-(3 * rows // (2 * fluids)) // 16) * 16
    lanes = -(-cap // 128) * 128
    slots = response.shape[1]
    width = span_dev // 2
    total = fluids * cap
    vmem = pl.BlockSpec(memory_space=pltpu.VMEM)
    smem = pl.BlockSpec(memory_space=pltpu.SMEM)
    anywhere = pl.BlockSpec(memory_space=pl.ANY)
    dma = pltpu.SemaphoreType.DMA
    out = pl.pallas_call(
        functools.partial(kernel, fluids, metals, cap),
        out_shape=[
            jax.ShapeDtypeStruct((slots, span_dev), f32),
            jax.ShapeDtypeStruct((slots, span_dev), f32),
            jax.ShapeDtypeStruct((rows, span_dev), f32),
        ],
        in_specs=[smem, anywhere, anywhere, vmem, vmem, vmem, anywhere, vmem, anywhere],
        out_specs=[anywhere] * 3,
        scratch_shapes=[
            pltpu.VMEM(fluid_temp.shape, bf16),
            pltpu.VMEM((rows, span_dev), f32),
            pltpu.VMEM(response.shape[1:], bf16),
            pltpu.VMEM((slots, span_dev), f32),
            pltpu.VMEM((total, rows), bf16),
            pltpu.VMEM((rows, total), bf16),
            pltpu.VMEM((slots, total), bf16),
            pltpu.VMEM((total, slots), bf16),
            pltpu.VMEM((fluids, 8, lanes), f32),
            pltpu.VMEM((fluids, 8, lanes), f32),
            pltpu.VMEM((2, fluids, cap, width), i16),
            pltpu.VMEM((2, fluids, cap, width), i16),
            pltpu.VMEM((2, 8, 128), f32),
            pltpu.VMEM((2, fluids, 8, 128), f32),
            pltpu.VMEM((2, metals, slots, width), bf16),
            pltpu.VMEM((2, slots, width), f32),
            pltpu.VMEM((slots, width), f32),
            pltpu.VMEM((2, fluids, cap, width), i16),
            pltpu.VMEM((2, fluids, cap, width), i16),
            pltpu.VMEM((2, 8, 128), f32),
            pltpu.VMEM((2, fluids, 8, 128), f32),
            pltpu.VMEM((2, rows, width), f32),
            pltpu.VMEM((rows, width), f32),
            pltpu.VMEM((slots, span_dev), f32),
            pltpu.VMEM((slots, span_dev), f32),
            pltpu.VMEM((rows, span_dev), f32),
            dma((7,)),
            dma((2, fluids)),
            dma((2, 2, fluids)),
            dma((2, 2, fluids)),
            dma((2, 2, metals)),
            dma((2, 2)),
            dma((2, 2, fluids)),
            dma((2, 2, fluids)),
        ],
        compiler_params=pltpu.CompilerParams(
            collective_id=0, has_side_effects=True, vmem_limit_bytes=48 * 1024 * 1024
        ),
    )(
        valid_rows,
        fluid_temp,
        wall_old.reshape(rows, span_dev),
        conductance,
        face_owner.reshape(blocks, cells),
        face_slot,
        response[0],
        coolant,
        flux_old[0],
    )
    return out[0][None], out[1][None], out[2].reshape(blocks, cells, span_dev)


def solution(mesh):
    in_specs = (
        P(("groups", "fluid", "metal"), None, None, "span"),
        P(("groups", "fluid", "metal"), None, "span"),
        P(("groups", "fluid", "metal"), None),
        P(("groups", "fluid", "metal")),
        P(("groups", "fluid", "metal"), None, None),
        P(("groups", "fluid", "metal"), None),
        P("fluid", "metal", None),
        P("fluid", "metal"),
        P(("groups", "fluid"), "metal", "span"),
    )
    out_specs = (
        P(("groups", "fluid"), "metal", "span"),
        P(("groups", "fluid"), "metal", "span"),
        P(("groups", "fluid", "metal"), None, "span"),
    )
    return jax.shard_map(body, mesh=mesh, in_specs=in_specs, out_specs=out_specs, check_vma=False)
```

```python
import functools

import jax
import jax.numpy as jnp
from jax import lax
from jax.experimental import pallas as pl
from jax.experimental.pallas import tpu as pltpu
from jax.sharding import PartitionSpec as P

average_weight = 0.3
span_mix = 0.25
relaxation = 0.5
code_limit = 32512.0
vmem_grant = 56 * 1024 * 1024
MESH = pl.DeviceIdType.MESH
f32, bf16, i32, i16 = jnp.float32, jnp.bfloat16, jnp.int32, jnp.int16


def mm(a, b):
    return jnp.dot(a, b, preferred_element_type=f32)


def to_column(row):
    eye = lax.broadcasted_iota(i32, (128, 128), 0) == lax.broadcasted_iota(i32, (128, 128), 1)
    return jnp.concatenate(
        [
            jnp.sum(jnp.where(eye, row[:, i : i + 128], 0.0), axis=1, keepdims=True)
            for i in range(0, row.shape[1], 128)
        ],
        axis=0,
    )


def encode(x):
    top = jnp.maximum(jnp.max(jnp.abs(x), keepdims=True), 1e-30)
    code = jnp.floor(x * (code_limit / top) + 0.5)
    return code, top * (1.0 / code_limit)


def code_parts(code):
    high = jnp.floor(code * (1.0 / 256.0) + 0.5)
    return jnp.concatenate([high, code - 256.0 * high], axis=1).astype(bf16)


def from_parts(both):
    half = both.shape[1] // 2
    return 256.0 * both[:, :half] + both[:, half:]


def value_parts(x):
    high = x.astype(bf16)
    return jnp.concatenate([high, (x - high.astype(f32)).astype(bf16)], axis=1)


def add_parts(both):
    half = both.shape[1] // 2
    return both[:, :half] + both[:, half:]


def pick(x, chunk):
    n = x.shape[1]
    if chunk == 0:
        return jnp.concatenate([x[:, 3 * n // 4 :], x[:, : n // 4]], axis=1)
    return x[:, n // 4 : 3 * n // 4]


def unpick(edge, middle):
    half = edge.shape[1] // 2
    return jnp.concatenate([edge[:, half:], middle, edge[:, :half]], axis=1)


def smooth(edge, middle, other):
    width = edge.shape[1]
    x = jnp.concatenate([edge, middle], axis=1)
    low = pltpu.roll(x, 1, 1)
    high = pltpu.roll(x, 2 * width - 1, 1)
    lane = lax.broadcasted_iota(i32, edge.shape, 1)
    low_edge = jnp.where(lane == width // 2, pltpu.roll(other, 1, 1), low[:, :width])
    high_edge = jnp.where(lane == width // 2 - 1, pltpu.roll(other, width - 1, 1), high[:, :width])
    new_edge = edge + span_mix * (high_edge - 2.0 * edge + low_edge)
    new_middle = middle + span_mix * (high[:, width:] - 2.0 * middle + low[:, width:])
    return unpick(new_edge, new_middle)


def kernel(
    fluids, metals, cap,
    valid_in, fluid_in, wall_in, cond_in, owner_in, slot_in, resp_in, cool_in, old_in,
    favg_out, mwall_out, wnew_out,
    favg_v, mwall_v, wnew_v, face_v, halo_f, wall_v, valid,
    cond, owner, slot, cool, fluid_v, resp_v, old_v,
    pack, unpack, spread, fetch,
    meta_s, meta_r, flux_s, flux_r, fstep_s, fstep_r,
    low_v, temp_v, halo_t, back_s, back_r, bstep_s, bstep_r,
    local_sem, meta_sem, flux_sem, fstep_sem, low_sem, halo_sem, back_sem, bstep_sem,
):
    blocks, layers, cells, span_dev = fluid_v.shape
    rows = blocks * cells
    slots = resp_v.shape[0]
    width = span_dev // 2
    me_f, me_m, me_s = lax.axis_index("fluid"), lax.axis_index("metal"), lax.axis_index("span")
    up = [None] + [lax.rem(me_f + r, fluids) for r in range(1, fluids)]
    down = [None] + [lax.rem(me_f + fluids - r, fluids) for r in range(1, fluids)]
    across = [None] + [lax.rem(me_m + r, metals) for r in range(1, metals)]
    mate = 1 - me_s

    loads = [
        pltpu.make_async_copy(src, dst, local_sem.at[i])
        for i, (src, dst) in enumerate(
            (
                (valid_in, valid), (owner_in, owner), (slot_in, slot), (fluid_in, fluid_v),
                (cond_in, cond), (wall_in, wall_v), (cool_in, cool), (old_in, old_v),
                (resp_in, resp_v),
            )
        )
    ]
    for load in loads:
        load.start()

    barrier = pltpu.get_barrier_semaphore()
    for r in range(1, fluids):
        pl.semaphore_signal(barrier, inc=1, device_id={"fluid": up[r]}, device_id_type=MESH)
    for r in range(1, metals):
        pl.semaphore_signal(barrier, inc=1, device_id={"metal": across[r]}, device_id_type=MESH)
    pl.semaphore_signal(barrier, inc=1, device_id={"span": mate}, device_id_type=MESH)

    def remote(src, dst, sems, place, where):
        return pltpu.make_async_remote_copy(
            src_ref=src, dst_ref=dst, send_sem=sems.at[(0, *place)], recv_sem=sems.at[(1, *place)],
            device_id=where, device_id_type=MESH,
        )

    for load in loads[:3]:
        load.wait()

    away = jnp.concatenate([owner[b : b + 1, :] for b in range(blocks)], axis=1) - me_f
    away = jnp.where(away < 0, away + fluids, away)
    cell = lax.broadcasted_iota(i32, (1, cells), 1)
    live = jnp.concatenate([(cell < valid[0:1, b : b + 1]).astype(i32) for b in range(blocks)], axis=1)
    away = jnp.where(live > 0, away, -1)
    lines = -(-fluids // 16) * 16
    chosen = lax.broadcasted_iota(i32, (lines, rows), 0) == away
    before = lax.broadcasted_iota(i32, (rows, rows), 0) < lax.broadcasted_iota(i32, (rows, rows), 1)
    earlier = mm(chosen.astype(f32).astype(bf16), before.astype(f32).astype(bf16))
    ordinal = jnp.sum(jnp.where(chosen, earlier, 0.0), axis=0, keepdims=True)
    place = jnp.where(away >= 0, away.astype(f32) * cap + ordinal, -1.0)
    total = fluids * cap
    pack[...] = (
        lax.broadcasted_iota(i32, (total, rows), 0).astype(f32) == place
    ).astype(f32).astype(bf16)
    place_col = to_column(place)
    unpack[...] = (
        lax.broadcasted_iota(i32, (rows, total), 1).astype(f32) == place_col
    ).astype(f32).astype(bf16)
    slot_row = jnp.concatenate([slot[b : b + 1, :] for b in range(blocks)], axis=1)
    line = lax.broadcasted_iota(i32, (16, rows), 0)
    halves = jnp.where(line == 0, slot_row // 256, jnp.where(line == 1, slot_row % 256, 0))
    packed_slots = mm(halves.astype(f32).astype(bf16), unpack[...])
    packed_slots = 256.0 * packed_slots[0:1] + packed_slots[1:2]
    for r in range(fluids):
        meta_s[r, :, 0:cap] = jnp.broadcast_to(packed_slots[:, r * cap : (r + 1) * cap], (8, cap))

    pl.semaphore_wait(barrier, fluids + metals - 1)
    sends = []

    def send(copy):
        copy.start()
        sends.append(copy)
        return copy

    metas = [
        send(remote(meta_s.at[r], meta_r.at[r], meta_sem, (r,), {"fluid": up[r]}))
        for r in range(1, fluids)
    ]

    for load in loads[3:6]:
        load.wait()
    weights = [2.0 * (layers - l) / (layers * (layers + 1.0)) for l in range(layers)]
    flux = []
    for b in range(blocks):
        near = weights[0] * fluid_v[b, 0].astype(f32)
        for l in range(1, layers):
            near = near + weights[l] * fluid_v[b, l].astype(f32)
        gain = to_column(cond[b : b + 1, :])
        lives = lax.broadcasted_iota(i32, (cells, 1), 0) < valid[0:1, b : b + 1]
        flux.append(
            jnp.where(lives, gain * (near - wall_v[b * cells : (b + 1) * cells, :]), 0.0)
        )
    flux = jnp.concatenate(flux, axis=0)

    fluxes, fsteps = [], []
    for c in range(2):
        code, step = encode(pick(flux, c))
        fstep_s[c] = jnp.broadcast_to(step, (8, 128))
        packed = from_parts(mm(pack[...], code_parts(code))).astype(i32).astype(i16)
        for r in range(fluids):
            dst = flux_r if r == 0 else flux_s
            dst[c, r] = packed[r * cap : (r + 1) * cap]
        fsteps.append(
            [
                send(remote(fstep_s.at[c], fstep_r.at[c, r], fstep_sem, (c, r), {"fluid": up[r]}))
                for r in range(1, fluids)
            ]
        )
        fluxes.append(
            [
                send(remote(flux_s.at[c, r], flux_r.at[c, r], flux_sem, (c, r), {"fluid": up[r]}))
                for r in range(1, fluids)
            ]
        )

    for copy in metas:
        copy.wait_recv()
    arrived = jnp.concatenate(
        [packed_slots[:, 0:cap]] + [meta_r[r, 0:1, 0:cap] for r in range(1, fluids)], axis=1
    )
    spread[...] = (
        lax.broadcasted_iota(i32, (slots, total), 0).astype(f32) == arrived
    ).astype(f32).astype(bf16)
    fetch[...] = (
        lax.broadcasted_iota(i32, (total, slots), 1).astype(f32) == to_column(arrived)
    ).astype(f32).astype(bf16)
    for load in loads[6:]:
        load.wait()
    cool_col = to_column(cool[...])

    averages, backs, bsteps = [], [], []
    for c in range(2):
        for copy in fsteps[c] + fluxes[c]:
            copy.wait_recv()
        incoming = jnp.concatenate(
            [
                flux_r[c, r].astype(i32).astype(f32)
                * (fstep_s[c, 0:1, :] if r == 0 else fstep_r[c, r, 0:1, :])
                for r in range(fluids)
            ],
            axis=0,
        )
        summed = add_parts(mm(spread[...], value_parts(incoming)))
        average = (1.0 - average_weight) * pick(old_v[...], c) + average_weight * summed
        averages.append(average)
        low_v[c, 0] = average.astype(bf16)
        lows = [
            send(remote(low_v.at[c, 0], low_v.at[c, r], low_sem, (c, r), {"metal": across[r]}))
            for r in range(1, metals)
        ]
        if c == 1:
            favg_v[...] = unpick(*averages)
            stores = [pltpu.make_async_copy(favg_v, favg_out, local_sem.at[9])]
            stores[0].start()
        temp = cool_col
        for r in range(metals):
            if r:
                lows[r - 1].wait_recv()
            stripe = lax.rem(me_m + metals - r, metals)
            columns = pl.ds(pl.multiple_of(stripe * slots, slots), slots)
            temp = temp + mm(resp_v[:, columns], low_v[c, r])
        temp_v[c] = temp
        if c == 0:
            edge_t = send(remote(temp_v.at[0], halo_t, halo_sem, (0,), {"span": mate}))
        code, step = encode(temp)
        bstep_s[c] = jnp.broadcast_to(step, (8, 128))
        found = from_parts(mm(fetch[...], code_parts(code))).astype(i32).astype(i16)
        for r in range(fluids):
            dst = back_r if r == 0 else back_s
            dst[c, r] = found[r * cap : (r + 1) * cap]
        bsteps.append(
            [
                send(remote(bstep_s.at[c], bstep_r.at[c, r], bstep_sem, (c, r), {"fluid": down[r]}))
                for r in range(1, fluids)
            ]
        )
        backs.append(
            [
                send(remote(back_s.at[c, r], back_r.at[c, r], back_sem, (c, r), {"fluid": down[r]}))
                for r in range(1, fluids)
            ]
        )

    edge_t.wait_recv()
    mwall_v[...] = smooth(temp_v[0], temp_v[1], halo_t[...])
    stores.append(pltpu.make_async_copy(mwall_v, mwall_out, local_sem.at[10]))
    stores[1].start()

    for c in range(2):
        for copy in bsteps[c] + backs[c]:
            copy.wait_recv()
        returned = jnp.concatenate(
            [
                back_r[c, r].astype(i32).astype(f32)
                * (bstep_s[c, 0:1, :] if r == 0 else bstep_r[c, r, 0:1, :])
                for r in range(fluids)
            ],
            axis=0,
        )
        face_v[c] = add_parts(mm(unpack[...], value_parts(returned)))
        if c == 0:
            edge_f = send(remote(face_v.at[0], halo_f, halo_sem, (1,), {"span": mate}))
    edge_f.wait_recv()
    for b in range(blocks):
        lives = lax.broadcasted_iota(i32, (cells, 1), 0) < valid[0:1, b : b + 1]
        part = pl.ds(b * cells, cells)
        face = smooth(face_v[0, part, :], face_v[1, part, :], halo_f[part, :])
        wnew_v[part, :] = jnp.where(
            lives, (1.0 - relaxation) * wall_v[part, :] + relaxation * face, 0.0
        )
        store = pltpu.make_async_copy(
            wnew_v.at[part, :], wnew_out.at[part, :], local_sem.at[11 + b]
        )
        store.start()
        stores.append(store)
    for copy in sends:
        copy.wait_send()
    for store in stores:
        store.wait()


def hand_over(*refs):
    count = (len(refs) - 1) // 2
    sem = refs[-1]
    copies = [
        pltpu.make_async_copy(refs[i], refs[count + i], sem.at[i]) for i in range(count)
    ]
    for copy in copies:
        copy.start()
    for copy in copies:
        copy.wait()


def body(
    fluid_temp, wall_old, conductance, valid_rows, face_owner, face_slot, response, coolant, flux_old
):
    blocks, layers, cells, span_dev = fluid_temp.shape
    rows = blocks * cells
    fluids, metals = lax.axis_size("fluid"), lax.axis_size("metal")
    cap = -(-(3 * rows // (2 * fluids)) // 16) * 16
    lanes = -(-cap // 128) * 128
    slots = response.shape[1]
    width = span_dev // 2
    total = fluids * cap
    hbm = pl.BlockSpec(memory_space=pltpu.HBM)
    dma = pltpu.SemaphoreType.DMA
    held = pl.pallas_call(
        functools.partial(kernel, fluids, metals, cap),
        out_shape=[
            jax.ShapeDtypeStruct((slots, span_dev), f32),
            jax.ShapeDtypeStruct((slots, span_dev), f32),
            jax.ShapeDtypeStruct((rows, span_dev), f32),
        ],
        in_specs=[hbm] * 9,
        out_specs=[hbm] * 3,
        scratch_shapes=[
            pltpu.VMEM((slots, span_dev), f32),
            pltpu.VMEM((slots, span_dev), f32),
            pltpu.VMEM((rows, span_dev), f32),
            pltpu.VMEM((2, rows, width), f32),
            pltpu.VMEM((rows, width), f32),
            pltpu.VMEM((rows, span_dev), f32),
            pltpu.VMEM((1, blocks), i32),
            pltpu.VMEM((blocks, cells), f32),
            pltpu.VMEM((blocks, cells), i32),
            pltpu.VMEM((blocks, cells), i32),
            pltpu.VMEM((1, slots), f32),
            pltpu.VMEM(fluid_temp.shape, bf16),
            pltpu.VMEM(response.shape[1:], bf16),
            pltpu.VMEM((slots, span_dev), f32),
            pltpu.VMEM((total, rows), bf16),
            pltpu.VMEM((rows, total), bf16),
            pltpu.VMEM((slots, total), bf16),
            pltpu.VMEM((total, slots), bf16),
            pltpu.VMEM((fluids, 8, lanes), f32),
            pltpu.VMEM((fluids, 8, lanes), f32),
            pltpu.VMEM((2, fluids, cap, width), i16),
            pltpu.VMEM((2, fluids, cap, width), i16),
            pltpu.VMEM((2, 8, 128), f32),
            pltpu.VMEM((2, fluids, 8, 128), f32),
            pltpu.VMEM((2, metals, slots, width), bf16),
            pltpu.VMEM((2, slots, width), f32),
            pltpu.VMEM((slots, width), f32),
            pltpu.VMEM((2, fluids, cap, width), i16),
            pltpu.VMEM((2, fluids, cap, width), i16),
            pltpu.VMEM((2, 8, 128), f32),
            pltpu.VMEM((2, fluids, 8, 128), f32),
            dma((11 + blocks,)),
            dma((2, fluids)),
            dma((2, 2, fluids)),
            dma((2, 2, fluids)),
            dma((2, 2, metals)),
            dma((2, 2)),
            dma((2, 2, fluids)),
            dma((2, 2, fluids)),
        ],
        compiler_params=pltpu.CompilerParams(
            collective_id=0, has_side_effects=True, vmem_limit_bytes=vmem_grant
        ),
    )(
        valid_rows.reshape(1, blocks),
        fluid_temp,
        wall_old.reshape(rows, span_dev),
        conductance,
        face_owner.reshape(blocks, cells),
        face_slot,
        response[0],
        coolant,
        flux_old[0],
    )
    out = pl.pallas_call(
        hand_over,
        out_shape=[jax.ShapeDtypeStruct(x.shape, x.dtype) for x in held],
        in_specs=[hbm] * 3,
        out_specs=[hbm] * 3,
        scratch_shapes=[dma((3,))],
        compiler_params=pltpu.CompilerParams(vmem_limit_bytes=vmem_grant),
    )(*held)
    return out[0][None], out[1][None], out[2].reshape(blocks, cells, span_dev)


def solution(mesh):
    in_specs = (
        P(("groups", "fluid", "metal"), None, None, "span"),
        P(("groups", "fluid", "metal"), None, "span"),
        P(("groups", "fluid", "metal"), None),
        P(("groups", "fluid", "metal")),
        P(("groups", "fluid", "metal"), None, None),
        P(("groups", "fluid", "metal"), None),
        P("fluid", "metal", None),
        P("fluid", "metal"),
        P(("groups", "fluid"), "metal", "span"),
    )
    out_specs = (
        P(("groups", "fluid"), "metal", "span"),
        P(("groups", "fluid"), "metal", "span"),
        P(("groups", "fluid", "metal"), None, "span"),
    )
    return jax.shard_map(body, mesh=mesh, in_specs=in_specs, out_specs=out_specs, check_vma=False)
```

```python
import functools

import jax
import jax.numpy as jnp
from jax import lax
from jax.experimental import pallas as pl
from jax.experimental.pallas import tpu as pltpu
from jax.sharding import PartitionSpec as P

average_weight = 0.3
span_mix = 0.25
relaxation = 0.5
code_limit = 32512.0
vmem_grant = 56 * 1024 * 1024
ln2 = 0.6931471805599453
MESH = pl.DeviceIdType.MESH
f32, bf16, i32, i16 = jnp.float32, jnp.bfloat16, jnp.int32, jnp.int16


def mm(a, b):
    return jnp.dot(a, b, preferred_element_type=f32)


def to_column(row):
    eye = lax.broadcasted_iota(i32, (128, 128), 0) == lax.broadcasted_iota(i32, (128, 128), 1)
    return jnp.concatenate(
        [
            jnp.sum(jnp.where(eye, row[:, i : i + 128], 0.0), axis=1, keepdims=True)
            for i in range(0, row.shape[1], 128)
        ],
        axis=0,
    )


def encode(x):
    top = jnp.maximum(jnp.max(jnp.abs(x), keepdims=True), 1e-30)
    level = jnp.floor(jnp.log(top) * (16.0 / ln2)) + 2.0
    return jnp.floor(x * (code_limit * jnp.exp(level * (-ln2 / 16.0))) + 0.5), level


def decode(block, cap):
    level = block[cap:].astype(i32).astype(f32)[0:1]
    return block[:cap].astype(i32).astype(f32) * (jnp.exp(level * (ln2 / 16.0)) * (1.0 / code_limit))


def fill(here, away, chunk, codes, level, cap):
    codes = codes.astype(i32).astype(i16)
    mark = jnp.broadcast_to(level, (16, codes.shape[1])).astype(i32).astype(i16)
    for r in range(codes.shape[0] // cap):
        dst = away if r else here
        dst[chunk, r, 0:cap] = codes[r * cap : (r + 1) * cap]
        dst[chunk, r, cap : cap + 16] = mark


def partner(me, r):
    for bit in range(r.bit_length()):
        if (r >> bit) & 1:
            me = me + (1 << bit) * (1 - 2 * ((me // (1 << bit)) % 2))
    return me


def code_parts(code):
    high = jnp.floor(code * (1.0 / 256.0) + 0.5)
    return jnp.concatenate([high, code - 256.0 * high], axis=1).astype(bf16)


def from_parts(both):
    half = both.shape[1] // 2
    return 256.0 * both[:, :half] + both[:, half:]


def value_parts(x):
    high = x.astype(bf16)
    return jnp.concatenate([high, (x - high.astype(f32)).astype(bf16)], axis=1)


def add_parts(both):
    half = both.shape[1] // 2
    return both[:, :half] + both[:, half:]


def pick(x, chunk):
    n = x.shape[1]
    if chunk == 0:
        return jnp.concatenate([x[:, 3 * n // 4 :], x[:, : n // 4]], axis=1)
    return x[:, n // 4 : 3 * n // 4]


def unpick(edge, middle):
    half = edge.shape[1] // 2
    return jnp.concatenate([edge[:, half:], middle, edge[:, :half]], axis=1)


def smooth(edge, middle, other):
    width = edge.shape[1]
    x = jnp.concatenate([edge, middle], axis=1)
    low = pltpu.roll(x, 1, 1)
    high = pltpu.roll(x, 2 * width - 1, 1)
    lane = lax.broadcasted_iota(i32, edge.shape, 1)
    low_edge = jnp.where(lane == width // 2, pltpu.roll(other, 1, 1), low[:, :width])
    high_edge = jnp.where(lane == width // 2 - 1, pltpu.roll(other, width - 1, 1), high[:, :width])
    new_edge = edge + span_mix * (high_edge - 2.0 * edge + low_edge)
    new_middle = middle + span_mix * (high[:, width:] - 2.0 * middle + low[:, width:])
    return unpick(new_edge, new_middle)


def kernel(
    fluids, metals, cap,
    valid_in, fluid_in, wall_in, cond_in, owner_in, slot_in, resp_in, cool_in, old_in,
    favg_out, mwall_out, wnew_out,
    favg_v, mwall_v, wnew_v, face_v, halo_f, wall_v, valid,
    cond, owner, slot, cool, fluid_v, resp_v, old_v,
    pack, unpack, spread, fetch,
    meta_s, meta_r, flux_s, flux_r,
    low_v, temp_v, halo_t, back_s, back_r,
    local_sem, meta_sem, flux_sem, low_sem, halo_sem, back_sem,
):
    blocks, layers, cells, span_dev = fluid_v.shape
    rows = blocks * cells
    slots = resp_v.shape[0]
    width = span_dev // 2
    me_f, me_m, me_s = lax.axis_index("fluid"), lax.axis_index("metal"), lax.axis_index("span")
    peers = [partner(me_f, r) for r in range(fluids)]
    order = list(range(fluids - 1, 0, -1))
    across = [None] + [lax.rem(me_m + r, metals) for r in range(1, metals)]
    mate = 1 - me_s

    loads = [
        pltpu.make_async_copy(src, dst, local_sem.at[i])
        for i, (src, dst) in enumerate(
            (
                (valid_in, valid), (owner_in, owner), (slot_in, slot), (fluid_in, fluid_v),
                (cond_in, cond), (wall_in, wall_v), (cool_in, cool), (old_in, old_v),
                (resp_in, resp_v),
            )
        )
    ]
    for load in loads:
        load.start()

    barrier = pltpu.get_barrier_semaphore()
    for r in order:
        pl.semaphore_signal(barrier, inc=1, device_id={"fluid": peers[r]}, device_id_type=MESH)
    for r in range(1, metals):
        pl.semaphore_signal(barrier, inc=1, device_id={"metal": across[r]}, device_id_type=MESH)
    pl.semaphore_signal(barrier, inc=1, device_id={"span": mate}, device_id_type=MESH)

    def remote(src, dst, sems, place, where):
        return pltpu.make_async_remote_copy(
            src_ref=src, dst_ref=dst, send_sem=sems.at[(0, *place)], recv_sem=sems.at[(1, *place)],
            device_id=where, device_id_type=MESH,
        )

    for load in loads[:3]:
        load.wait()

    away = jnp.concatenate([owner[b : b + 1, :] for b in range(blocks)], axis=1) ^ me_f
    cell = lax.broadcasted_iota(i32, (1, cells), 1)
    live = jnp.concatenate([(cell < valid[0:1, b : b + 1]).astype(i32) for b in range(blocks)], axis=1)
    away = jnp.where(live > 0, away, -1)
    lines = -(-fluids // 16) * 16
    chosen = lax.broadcasted_iota(i32, (lines, rows), 0) == away
    before = lax.broadcasted_iota(i32, (rows, rows), 0) < lax.broadcasted_iota(i32, (rows, rows), 1)
    earlier = mm(chosen.astype(f32).astype(bf16), before.astype(f32).astype(bf16))
    ordinal = jnp.sum(jnp.where(chosen, earlier, 0.0), axis=0, keepdims=True)
    place = jnp.where(away >= 0, away.astype(f32) * cap + ordinal, -1.0)
    total = fluids * cap
    pack[...] = (
        lax.broadcasted_iota(i32, (total, rows), 0).astype(f32) == place
    ).astype(f32).astype(bf16)
    slot_row = jnp.concatenate([slot[b : b + 1, :] for b in range(blocks)], axis=1)
    line = lax.broadcasted_iota(i32, (16, rows), 0)
    halves = jnp.where(line == 0, slot_row // 256, jnp.where(line == 1, slot_row % 256, 0))
    packed_slots = lax.dot_general(
        halves.astype(f32).astype(bf16), pack[...], (((1,), (1,)), ((), ())),
        preferred_element_type=f32,
    )
    packed_slots = 256.0 * packed_slots[0:1] + packed_slots[1:2]
    for r in range(fluids):
        meta_s[r, :, 0:cap] = jnp.broadcast_to(packed_slots[:, r * cap : (r + 1) * cap], (8, cap))

    pl.semaphore_wait(barrier, fluids + metals - 1)
    sends = []

    def send(copy):
        copy.start()
        sends.append(copy)
        return copy

    metas = [
        send(remote(meta_s.at[r], meta_r.at[r], meta_sem, (r,), {"fluid": peers[r]}))
        for r in order
    ]

    for load in loads[3:6]:
        load.wait()
    weights = [2.0 * (layers - l) / (layers * (layers + 1.0)) for l in range(layers)]
    flux = []
    for b in range(blocks):
        near = weights[0] * fluid_v[b, 0].astype(f32)
        for l in range(1, layers):
            near = near + weights[l] * fluid_v[b, l].astype(f32)
        gain = to_column(cond[b : b + 1, :])
        lives = lax.broadcasted_iota(i32, (cells, 1), 0) < valid[0:1, b : b + 1]
        flux.append(
            jnp.where(lives, gain * (near - wall_v[b * cells : (b + 1) * cells, :]), 0.0)
        )
    flux = jnp.concatenate(flux, axis=0)

    fluxes = []
    for c in range(2):
        code, level = encode(pick(flux, c))
        fill(flux_r, flux_s, c, from_parts(mm(pack[...], code_parts(code))), level, cap)
        fluxes.append(
            [
                send(remote(flux_s.at[c, r], flux_r.at[c, r], flux_sem, (c, r), {"fluid": peers[r]}))
                for r in order
            ]
        )
    unpack[...] = (
        lax.broadcasted_iota(i32, (rows, total), 1).astype(f32) == to_column(place)
    ).astype(f32).astype(bf16)

    for copy in metas:
        copy.wait_recv()
    arrived = jnp.concatenate(
        [packed_slots[:, 0:cap]] + [meta_r[r, 0:1, 0:cap] for r in range(1, fluids)], axis=1
    )
    spread[...] = (
        lax.broadcasted_iota(i32, (slots, total), 0).astype(f32) == arrived
    ).astype(f32).astype(bf16)
    fetch[...] = (
        lax.broadcasted_iota(i32, (total, slots), 1).astype(f32) == to_column(arrived)
    ).astype(f32).astype(bf16)
    for load in loads[6:]:
        load.wait()
    cool_col = to_column(cool[...])

    averages, backs = [], []
    for c in range(2):
        for copy in fluxes[c]:
            copy.wait_recv()
        incoming = jnp.concatenate(
            [decode(flux_r[c, r], cap) for r in range(fluids)], axis=0
        )
        summed = add_parts(mm(spread[...], value_parts(incoming)))
        average = (1.0 - average_weight) * pick(old_v[...], c) + average_weight * summed
        averages.append(average)
        low_v[c, 0] = average.astype(bf16)
        lows = [
            send(remote(low_v.at[c, 0], low_v.at[c, r], low_sem, (c, r), {"metal": across[r]}))
            for r in range(1, metals)
        ]
        if c == 1:
            favg_v[...] = unpick(*averages)
            stores = [pltpu.make_async_copy(favg_v, favg_out, local_sem.at[9])]
            stores[0].start()
        temp = cool_col
        for r in range(metals):
            if r:
                lows[r - 1].wait_recv()
            stripe = lax.rem(me_m + metals - r, metals)
            columns = pl.ds(pl.multiple_of(stripe * slots, slots), slots)
            temp = temp + mm(resp_v[:, columns], low_v[c, r])
        temp_v[c] = temp
        if c == 0:
            edge_t = send(remote(temp_v.at[0], halo_t, halo_sem, (0,), {"span": mate}))
        code, level = encode(temp)
        fill(back_r, back_s, c, from_parts(mm(fetch[...], code_parts(code))), level, cap)
        backs.append(
            [
                send(remote(back_s.at[c, r], back_r.at[c, r], back_sem, (c, r), {"fluid": peers[r]}))
                for r in order
            ]
        )

    edge_t.wait_recv()
    mwall_v[...] = smooth(temp_v[0], temp_v[1], halo_t[...])
    stores.append(pltpu.make_async_copy(mwall_v, mwall_out, local_sem.at[10]))
    stores[1].start()

    for c in range(2):
        for copy in backs[c]:
            copy.wait_recv()
        returned = jnp.concatenate(
            [decode(back_r[c, r], cap) for r in range(fluids)], axis=0
        )
        face_v[c] = add_parts(mm(unpack[...], value_parts(returned)))
        if c == 0:
            edge_f = send(remote(face_v.at[0], halo_f, halo_sem, (1,), {"span": mate}))
    edge_f.wait_recv()
    for b in range(blocks):
        lives = lax.broadcasted_iota(i32, (cells, 1), 0) < valid[0:1, b : b + 1]
        part = pl.ds(b * cells, cells)
        face = smooth(face_v[0, part, :], face_v[1, part, :], halo_f[part, :])
        wnew_v[part, :] = jnp.where(
            lives, (1.0 - relaxation) * wall_v[part, :] + relaxation * face, 0.0
        )
        store = pltpu.make_async_copy(
            wnew_v.at[part, :], wnew_out.at[part, :], local_sem.at[11 + b]
        )
        store.start()
        stores.append(store)
    for copy in sends:
        copy.wait_send()
    for store in stores:
        store.wait()


def hand_over(*refs):
    count = (len(refs) - 2) // 3
    sources, targets, held, (load_sem, store_sem) = (
        refs[:count], refs[count : 2 * count], refs[2 * count : 3 * count], refs[3 * count :]
    )
    loads = [pltpu.make_async_copy(sources[i], held[i], load_sem.at[i]) for i in range(count)]
    stores = [pltpu.make_async_copy(held[i], targets[i], store_sem.at[i]) for i in range(count)]
    for load in loads:
        load.start()
    for load, store in zip(loads, stores):
        load.wait()
        store.start()
    for store in stores:
        store.wait()


def body(
    fluid_temp, wall_old, conductance, valid_rows, face_owner, face_slot, response, coolant, flux_old
):
    blocks, layers, cells, span_dev = fluid_temp.shape
    rows = blocks * cells
    fluids, metals = lax.axis_size("fluid"), lax.axis_size("metal")
    cap = -(-(3 * rows // (2 * fluids)) // 16) * 16
    lanes = -(-cap // 128) * 128
    slots = response.shape[1]
    width = span_dev // 2
    total = fluids * cap
    hbm = pl.BlockSpec(memory_space=pltpu.HBM)
    dma = pltpu.SemaphoreType.DMA
    held = pl.pallas_call(
        functools.partial(kernel, fluids, metals, cap),
        out_shape=[
            jax.ShapeDtypeStruct((slots, span_dev), f32),
            jax.ShapeDtypeStruct((slots, span_dev), f32),
            jax.ShapeDtypeStruct((rows, span_dev), f32),
        ],
        in_specs=[hbm] * 9,
        out_specs=[hbm] * 3,
        scratch_shapes=[
            pltpu.VMEM((slots, span_dev), f32),
            pltpu.VMEM((slots, span_dev), f32),
            pltpu.VMEM((rows, span_dev), f32),
            pltpu.VMEM((2, rows, width), f32),
            pltpu.VMEM((rows, width), f32),
            pltpu.VMEM((rows, span_dev), f32),
            pltpu.VMEM((1, blocks), i32),
            pltpu.VMEM((blocks, cells), f32),
            pltpu.VMEM((blocks, cells), i32),
            pltpu.VMEM((blocks, cells), i32),
            pltpu.VMEM((1, slots), f32),
            pltpu.VMEM(fluid_temp.shape, bf16),
            pltpu.VMEM(response.shape[1:], bf16),
            pltpu.VMEM((slots, span_dev), f32),
            pltpu.VMEM((total, rows), bf16),
            pltpu.VMEM((rows, total), bf16),
            pltpu.VMEM((slots, total), bf16),
            pltpu.VMEM((total, slots), bf16),
            pltpu.VMEM((fluids, 8, lanes), f32),
            pltpu.VMEM((fluids, 8, lanes), f32),
            pltpu.VMEM((2, fluids, cap + 16, width), i16),
            pltpu.VMEM((2, fluids, cap + 16, width), i16),
            pltpu.VMEM((2, metals, slots, width), bf16),
            pltpu.VMEM((2, slots, width), f32),
            pltpu.VMEM((slots, width), f32),
            pltpu.VMEM((2, fluids, cap + 16, width), i16),
            pltpu.VMEM((2, fluids, cap + 16, width), i16),
            dma((11 + blocks,)),
            dma((2, fluids)),
            dma((2, 2, fluids)),
            dma((2, 2, metals)),
            dma((2, 2)),
            dma((2, 2, fluids)),
        ],
        compiler_params=pltpu.CompilerParams(
            collective_id=0, has_side_effects=True, vmem_limit_bytes=vmem_grant
        ),
    )(
        valid_rows.reshape(1, blocks),
        fluid_temp,
        wall_old.reshape(rows, span_dev),
        conductance,
        face_owner.reshape(blocks, cells),
        face_slot,
        response[0],
        coolant,
        flux_old[0],
    )
    out = pl.pallas_call(
        hand_over,
        out_shape=[jax.ShapeDtypeStruct(x.shape, x.dtype) for x in held],
        in_specs=[hbm] * 3,
        out_specs=[hbm] * 3,
        scratch_shapes=[pltpu.VMEM(x.shape, x.dtype) for x in held] + [dma((3,)), dma((3,))],
        compiler_params=pltpu.CompilerParams(vmem_limit_bytes=vmem_grant),
    )(*held)
    return out[0][None], out[1][None], out[2].reshape(blocks, cells, span_dev)


def solution(mesh):
    in_specs = (
        P(("groups", "fluid", "metal"), None, None, "span"),
        P(("groups", "fluid", "metal"), None, "span"),
        P(("groups", "fluid", "metal"), None),
        P(("groups", "fluid", "metal")),
        P(("groups", "fluid", "metal"), None, None),
        P(("groups", "fluid", "metal"), None),
        P("fluid", "metal", None),
        P("fluid", "metal"),
        P(("groups", "fluid"), "metal", "span"),
    )
    out_specs = (
        P(("groups", "fluid"), "metal", "span"),
        P(("groups", "fluid"), "metal", "span"),
        P(("groups", "fluid", "metal"), None, "span"),
    )
    return jax.shard_map(body, mesh=mesh, in_specs=in_specs, out_specs=out_specs, check_vma=False)
```

```python
import functools

import jax
import jax.numpy as jnp
from jax import lax
from jax.experimental import pallas as pl
from jax.experimental.pallas import tpu as pltpu
from jax.sharding import PartitionSpec as P

average_weight = 0.3
span_mix = 0.25
relaxation = 0.5
code_limit = 32512.0
vmem_grant = 56 * 1024 * 1024
ln2 = 0.6931471805599453
MESH = pl.DeviceIdType.MESH
f32, bf16, i32, i16 = jnp.float32, jnp.bfloat16, jnp.int32, jnp.int16


def mm(a, b):
    return jnp.dot(a, b, preferred_element_type=f32)


def to_column(row):
    eye = lax.broadcasted_iota(i32, (128, 128), 0) == lax.broadcasted_iota(i32, (128, 128), 1)
    return jnp.concatenate(
        [
            jnp.sum(jnp.where(eye, row[:, i : i + 128], 0.0), axis=1, keepdims=True)
            for i in range(0, row.shape[1], 128)
        ],
        axis=0,
    )


def encode(x):
    top = jnp.maximum(jnp.max(jnp.abs(x), keepdims=True), 1e-30)
    level = jnp.floor(jnp.log(top) * (16.0 / ln2)) + 2.0
    return jnp.floor(x * (code_limit * jnp.exp(level * (-ln2 / 16.0))) + 0.5), level


def decode(codes, level):
    return codes.astype(i32).astype(f32) * (jnp.exp(level * (ln2 / 16.0)) * (1.0 / code_limit))


def fill(here, away, chunk, codes, cap):
    codes = codes.astype(i32).astype(i16)
    for r in range(codes.shape[0] // cap):
        dst = away if r else here
        dst[chunk, r] = codes[r * cap : (r + 1) * cap]


def partner(me, r):
    for bit in range(r.bit_length()):
        if (r >> bit) & 1:
            me = me + (1 << bit) * (1 - 2 * ((me // (1 << bit)) % 2))
    return me


def code_parts(code):
    high = jnp.floor(code * (1.0 / 256.0) + 0.5)
    return jnp.concatenate([high, code - 256.0 * high], axis=1).astype(bf16)


def from_parts(both):
    half = both.shape[1] // 2
    return 256.0 * both[:, :half] + both[:, half:]


def value_parts(x):
    high = x.astype(bf16)
    return jnp.concatenate([high, (x - high.astype(f32)).astype(bf16)], axis=1)


def add_parts(both):
    half = both.shape[1] // 2
    return both[:, :half] + both[:, half:]


def pick(x, chunk):
    n = x.shape[1]
    if chunk == 0:
        return jnp.concatenate([x[:, 3 * n // 4 :], x[:, : n // 4]], axis=1)
    return x[:, n // 4 : 3 * n // 4]


def unpick(edge, middle):
    half = edge.shape[1] // 2
    return jnp.concatenate([edge[:, half:], middle, edge[:, :half]], axis=1)


def smooth(edge, middle, other):
    width = edge.shape[1]
    x = jnp.concatenate([edge, middle], axis=1)
    low = pltpu.roll(x, 1, 1)
    high = pltpu.roll(x, 2 * width - 1, 1)
    lane = lax.broadcasted_iota(i32, edge.shape, 1)
    low_edge = jnp.where(lane == width // 2, pltpu.roll(other, 1, 1), low[:, :width])
    high_edge = jnp.where(lane == width // 2 - 1, pltpu.roll(other, width - 1, 1), high[:, :width])
    new_edge = edge + span_mix * (high_edge - 2.0 * edge + low_edge)
    new_middle = middle + span_mix * (high[:, width:] - 2.0 * middle + low[:, width:])
    return unpick(new_edge, new_middle)


def kernel(
    fluids, metals, cap,
    valid_in, fluid_in, wall_in, cond_in, owner_in, slot_in, resp_in, cool_in, old_in,
    favg_out, mwall_out, wnew_out,
    favg_v, mwall_v, wnew_v, face_v, halo_f, wall_v, valid,
    cond, owner, slot, cool, fluid_v, resp_v, old_v,
    pack, unpack, spread, fetch,
    meta_s, meta_r, flux_s, flux_r,
    low_v, temp_v, halo_t, back_s, back_r, blevel_s, blevel_r,
    local_sem, meta_sem, flux_sem, low_sem, halo_sem, back_sem, blevel_sem,
):
    blocks, layers, cells, span_dev = fluid_v.shape
    rows = blocks * cells
    slots = resp_v.shape[0]
    width = span_dev // 2
    me_f, me_m, me_s = lax.axis_index("fluid"), lax.axis_index("metal"), lax.axis_index("span")
    peers = [partner(me_f, r) for r in range(fluids)]
    order = list(range(fluids - 1, 0, -1))
    across = [None] + [lax.rem(me_m + r, metals) for r in range(1, metals)]
    mate = 1 - me_s

    loads = [
        pltpu.make_async_copy(src, dst, local_sem.at[i])
        for i, (src, dst) in enumerate(
            (
                (valid_in, valid), (owner_in, owner), (slot_in, slot), (cond_in, cond),
                (wall_in, wall_v), (cool_in, cool), (old_in, old_v), (resp_in, resp_v),
            )
        )
    ]
    fluid_loads = [
        pltpu.make_async_copy(fluid_in.at[b], fluid_v.at[b], local_sem.at[11 + blocks + b])
        for b in range(blocks)
    ]
    for load in loads[:4] + fluid_loads + loads[4:5]:
        load.start()

    barrier = pltpu.get_barrier_semaphore()
    for r in order:
        pl.semaphore_signal(barrier, inc=1, device_id={"fluid": peers[r]}, device_id_type=MESH)
    for r in range(1, metals):
        pl.semaphore_signal(barrier, inc=1, device_id={"metal": across[r]}, device_id_type=MESH)
    pl.semaphore_signal(barrier, inc=1, device_id={"span": mate}, device_id_type=MESH)

    def remote(src, dst, sems, place, where):
        return pltpu.make_async_remote_copy(
            src_ref=src, dst_ref=dst, send_sem=sems.at[(0, *place)], recv_sem=sems.at[(1, *place)],
            device_id=where, device_id_type=MESH,
        )

    for load in loads[:3]:
        load.wait()

    away = jnp.concatenate([owner[b : b + 1, :] for b in range(blocks)], axis=1) ^ me_f
    cell = lax.broadcasted_iota(i32, (1, cells), 1)
    live = jnp.concatenate([(cell < valid[0:1, b : b + 1]).astype(i32) for b in range(blocks)], axis=1)
    away = jnp.where(live > 0, away, -1)
    lines = -(-fluids // 16) * 16
    chosen = lax.broadcasted_iota(i32, (lines, rows), 0) == away
    before = lax.broadcasted_iota(i32, (rows, rows), 0) < lax.broadcasted_iota(i32, (rows, rows), 1)
    earlier = mm(chosen.astype(f32).astype(bf16), before.astype(f32).astype(bf16))
    ordinal = jnp.sum(jnp.where(chosen, earlier, 0.0), axis=0, keepdims=True)
    place = jnp.where(away >= 0, away.astype(f32) * cap + ordinal, -1.0)
    total = fluids * cap
    pack[...] = (
        lax.broadcasted_iota(i32, (total, rows), 0).astype(f32) == place
    ).astype(f32).astype(bf16)
    slot_row = jnp.concatenate([slot[b : b + 1, :] for b in range(blocks)], axis=1)
    line = lax.broadcasted_iota(i32, (16, rows), 0)
    halves = jnp.where(line == 0, slot_row // 256, jnp.where(line == 1, slot_row % 256, 0))
    packed_slots = lax.dot_general(
        halves.astype(f32).astype(bf16), pack[...], (((1,), (1,)), ((), ())),
        preferred_element_type=f32,
    )
    packed_slots = 256.0 * packed_slots[0:1] + packed_slots[1:2]
    for load in loads[3:5]:
        load.wait()
    weights = [2.0 * (layers - l) / (layers * (layers + 1.0)) for l in range(layers)]
    flux = []
    for b in range(blocks):
        fluid_loads[b].wait()
        near = weights[0] * fluid_v[b, 0].astype(f32)
        for l in range(1, layers):
            near = near + weights[l] * fluid_v[b, l].astype(f32)
        gain = to_column(cond[b : b + 1, :])
        lives = lax.broadcasted_iota(i32, (cells, 1), 0) < valid[0:1, b : b + 1]
        flux.append(
            jnp.where(lives, gain * (near - wall_v[b * cells : (b + 1) * cells, :]), 0.0)
        )
    flux = jnp.concatenate(flux, axis=0)
    for load in loads[5:]:
        load.start()

    flux, level = encode(flux)
    lanes = meta_s.shape[2] - width
    for r in range(fluids):
        meta_s[r, :, 0:cap] = packed_slots[:, r * cap : (r + 1) * cap]
        meta_s[r, :, lanes:] = jnp.broadcast_to(level, (1, width))

    pl.semaphore_wait(barrier, fluids + metals - 1)
    sends = []

    def send(copy):
        copy.start()
        sends.append(copy)
        return copy

    metas = [
        send(remote(meta_s.at[r], meta_r.at[r], meta_sem, (r,), {"fluid": peers[r]}))
        for r in order
    ]

    fluxes = []
    for c in range(2):
        fill(flux_r, flux_s, c, from_parts(mm(pack[...], code_parts(pick(flux, c)))), cap)
        fluxes.append(
            [
                send(remote(flux_s.at[c, r], flux_r.at[c, r], flux_sem, (c, r), {"fluid": peers[r]}))
                for r in order
            ]
        )
    unpack[...] = (
        lax.broadcasted_iota(i32, (rows, total), 1).astype(f32) == to_column(place)
    ).astype(f32).astype(bf16)

    for copy in metas:
        copy.wait_recv()
    arrived = jnp.concatenate(
        [packed_slots[:, 0:cap]] + [meta_r[r, :, 0:cap] for r in range(1, fluids)], axis=1
    )
    spread[...] = (
        lax.broadcasted_iota(i32, (slots, total), 0).astype(f32) == arrived
    ).astype(f32).astype(bf16)
    fetch[...] = (
        lax.broadcasted_iota(i32, (total, slots), 1).astype(f32) == to_column(arrived)
    ).astype(f32).astype(bf16)
    for load in loads[5:]:
        load.wait()
    cool_col = to_column(cool[...])

    averages, lows, backs = [], [], []
    for c in range(2):
        for copy in fluxes[c]:
            copy.wait_recv()
        incoming = jnp.concatenate(
            [
                decode(flux_r[c, r], (meta_r if r else meta_s)[r, :, lanes:])
                for r in range(fluids)
            ], axis=0
        )
        summed = add_parts(mm(spread[...], value_parts(incoming)))
        average = (1.0 - average_weight) * pick(old_v[...], c) + average_weight * summed
        averages.append(average)
        low_v[c, 0] = average.astype(bf16)
        lows.append(
            [
                send(remote(low_v.at[c, 0], low_v.at[c, r], low_sem, (c, r), {"metal": across[r]}))
                for r in range(1, metals)
            ]
        )
    for c in range(2):
        temp = cool_col
        for r in range(metals):
            if r:
                lows[c][r - 1].wait_recv()
            stripe = lax.rem(me_m + metals - r, metals)
            columns = pl.ds(pl.multiple_of(stripe * slots, slots), slots)
            temp = temp + mm(resp_v[:, columns], low_v[c, r])
        temp_v[c] = temp
        if c == 0:
            edge_t = send(remote(temp_v.at[0], halo_t, halo_sem, (0,), {"span": mate}))
        code, level = encode(temp)
        blevel_s[c] = jnp.broadcast_to(level, (1, width))
        fill(back_r, back_s, c, from_parts(mm(fetch[...], code_parts(code))), cap)
        backs.append(
            [
                send(remote(blevel_s.at[c], blevel_r.at[c, r], blevel_sem, (c, r), {"fluid": peers[r]}))
                for r in order
            ]
            + [
                send(remote(back_s.at[c, r], back_r.at[c, r], back_sem, (c, r), {"fluid": peers[r]}))
                for r in order
            ]
        )

    favg_v[...] = unpick(*averages)
    stores = [pltpu.make_async_copy(favg_v, favg_out, local_sem.at[9])]
    stores[0].start()
    edge_t.wait_recv()
    mwall_v[...] = smooth(temp_v[0], temp_v[1], halo_t[...])
    stores.append(pltpu.make_async_copy(mwall_v, mwall_out, local_sem.at[10]))
    stores[1].start()

    for c in range(2):
        for copy in backs[c]:
            copy.wait_recv()
        returned = jnp.concatenate(
            [
                decode(back_r[c, r], blevel_r[c, r] if r else blevel_s[c])
                for r in range(fluids)
            ], axis=0
        )
        face_v[c] = add_parts(mm(unpack[...], value_parts(returned)))
        if c == 0:
            edge_f = send(remote(face_v.at[0], halo_f, halo_sem, (1,), {"span": mate}))
    edge_f.wait_recv()
    for b in range(blocks):
        lives = lax.broadcasted_iota(i32, (cells, 1), 0) < valid[0:1, b : b + 1]
        part = pl.ds(b * cells, cells)
        face = smooth(face_v[0, part, :], face_v[1, part, :], halo_f[part, :])
        wnew_v[part, :] = jnp.where(
            lives, (1.0 - relaxation) * wall_v[part, :] + relaxation * face, 0.0
        )
        store = pltpu.make_async_copy(
            wnew_v.at[part, :], wnew_out.at[part, :], local_sem.at[11 + b]
        )
        store.start()
        stores.append(store)
    for copy in sends:
        copy.wait_send()
    for store in stores:
        store.wait()


def hand_over(*refs):
    count = (len(refs) - 2) // 3
    sources, targets, held, (load_sem, store_sem) = (
        refs[:count], refs[count : 2 * count], refs[2 * count : 3 * count], refs[3 * count :]
    )
    loads = [pltpu.make_async_copy(sources[i], held[i], load_sem.at[i]) for i in range(count)]
    stores = [pltpu.make_async_copy(held[i], targets[i], store_sem.at[i]) for i in range(count)]
    for load in loads:
        load.start()
    for load, store in zip(loads, stores):
        load.wait()
        store.start()
    for store in stores:
        store.wait()


def body(
    fluid_temp, wall_old, conductance, valid_rows, face_owner, face_slot, response, coolant, flux_old
):
    blocks, layers, cells, span_dev = fluid_temp.shape
    rows = blocks * cells
    fluids, metals = lax.axis_size("fluid"), lax.axis_size("metal")
    cap = -(-(3 * rows // (2 * fluids)) // 16) * 16
    lanes = -(-cap // 128) * 128
    slots = response.shape[1]
    width = span_dev // 2
    total = fluids * cap
    hbm = pl.BlockSpec(memory_space=pltpu.HBM)
    dma = pltpu.SemaphoreType.DMA
    held = pl.pallas_call(
        functools.partial(kernel, fluids, metals, cap),
        out_shape=[
            jax.ShapeDtypeStruct((slots, span_dev), f32),
            jax.ShapeDtypeStruct((slots, span_dev), f32),
            jax.ShapeDtypeStruct((rows, span_dev), f32),
        ],
        in_specs=[hbm] * 9,
        out_specs=[hbm] * 3,
        scratch_shapes=[
            pltpu.VMEM((slots, span_dev), f32),
            pltpu.VMEM((slots, span_dev), f32),
            pltpu.VMEM((rows, span_dev), f32),
            pltpu.VMEM((2, rows, width), f32),
            pltpu.VMEM((rows, width), f32),
            pltpu.VMEM((rows, span_dev), f32),
            pltpu.VMEM((1, blocks), i32),
            pltpu.VMEM((blocks, cells), f32),
            pltpu.VMEM((blocks, cells), i32),
            pltpu.VMEM((blocks, cells), i32),
            pltpu.VMEM((1, slots), f32),
            pltpu.VMEM(fluid_temp.shape, bf16),
            pltpu.VMEM(response.shape[1:], bf16),
            pltpu.VMEM((slots, span_dev), f32),
            pltpu.VMEM((total, rows), bf16),
            pltpu.VMEM((rows, total), bf16),
            pltpu.VMEM((slots, total), bf16),
            pltpu.VMEM((total, slots), bf16),
            pltpu.VMEM((fluids, 1, lanes + width), f32),
            pltpu.VMEM((fluids, 1, lanes + width), f32),
            pltpu.VMEM((2, fluids, cap, width), i16),
            pltpu.VMEM((2, fluids, cap, width), i16),
            pltpu.VMEM((2, metals, slots, width), bf16),
            pltpu.VMEM((2, slots, width), f32),
            pltpu.VMEM((slots, width), f32),
            pltpu.VMEM((2, fluids, cap, width), i16),
            pltpu.VMEM((2, fluids, cap, width), i16),
            pltpu.VMEM((2, 1, width), f32),
            pltpu.VMEM((2, fluids, 1, width), f32),
            dma((11 + 2 * blocks,)),
            dma((2, fluids)),
            dma((2, 2, fluids)),
            dma((2, 2, metals)),
            dma((2, 2)),
            dma((2, 2, fluids)),
            dma((2, 2, fluids)),
        ],
        compiler_params=pltpu.CompilerParams(
            collective_id=0, has_side_effects=True, vmem_limit_bytes=vmem_grant
        ),
    )(
        valid_rows.reshape(1, blocks),
        fluid_temp,
        wall_old.reshape(rows, span_dev),
        conductance,
        face_owner.reshape(blocks, cells),
        face_slot,
        response[0],
        coolant,
        flux_old[0],
    )
    out = pl.pallas_call(
        hand_over,
        out_shape=[jax.ShapeDtypeStruct(x.shape, x.dtype) for x in held],
        in_specs=[hbm] * 3,
        out_specs=[hbm] * 3,
        scratch_shapes=[pltpu.VMEM(x.shape, x.dtype) for x in held] + [dma((3,)), dma((3,))],
        compiler_params=pltpu.CompilerParams(vmem_limit_bytes=vmem_grant),
    )(*held)
    return out[0][None], out[1][None], out[2].reshape(blocks, cells, span_dev)


def solution(mesh):
    in_specs = (
        P(("groups", "fluid", "metal"), None, None, "span"),
        P(("groups", "fluid", "metal"), None, "span"),
        P(("groups", "fluid", "metal"), None),
        P(("groups", "fluid", "metal")),
        P(("groups", "fluid", "metal"), None, None),
        P(("groups", "fluid", "metal"), None),
        P("fluid", "metal", None),
        P("fluid", "metal"),
        P(("groups", "fluid"), "metal", "span"),
    )
    out_specs = (
        P(("groups", "fluid"), "metal", "span"),
        P(("groups", "fluid"), "metal", "span"),
        P(("groups", "fluid", "metal"), None, "span"),
    )
    return jax.shard_map(body, mesh=mesh, in_specs=in_specs, out_specs=out_specs, check_vma=False)
```

```python
import functools

import jax
import jax.numpy as jnp
from jax import lax
from jax.experimental import pallas as pl
from jax.experimental.pallas import tpu as pltpu
from jax.sharding import PartitionSpec as P

average_weight = 0.3
span_mix = 0.25
relaxation = 0.5
code_limit = 32512.0
vmem_grant = 56 * 1024 * 1024
ln2 = 0.6931471805599453
MESH = pl.DeviceIdType.MESH
f32, bf16, i32, i16 = jnp.float32, jnp.bfloat16, jnp.int32, jnp.int16


def mm(a, b):
    return jnp.dot(a, b, preferred_element_type=f32)


def to_column(row):
    eye = lax.broadcasted_iota(i32, (128, 128), 0) == lax.broadcasted_iota(i32, (128, 128), 1)
    return jnp.concatenate(
        [
            jnp.sum(jnp.where(eye, row[:, i : i + 128], 0.0), axis=1, keepdims=True)
            for i in range(0, row.shape[1], 128)
        ],
        axis=0,
    )


def encode(x):
    top = jnp.maximum(jnp.max(jnp.abs(x), keepdims=True), 1e-30)
    level = jnp.floor(jnp.log(top) * (16.0 / ln2)) + 2.0
    return jnp.floor(x * (code_limit * jnp.exp(level * (-ln2 / 16.0))) + 0.5), level


def decode(codes, level):
    return codes.astype(i32).astype(f32) * (jnp.exp(level * (ln2 / 16.0)) * (1.0 / code_limit))


def fill(here, away, chunk, codes, cap):
    codes = codes.astype(i32).astype(i16)
    for r in range(codes.shape[0] // cap):
        dst = away if r else here
        dst[chunk, r] = codes[r * cap : (r + 1) * cap]


def partner(me, r):
    for bit in range(r.bit_length()):
        if (r >> bit) & 1:
            me = me + (1 << bit) * (1 - 2 * ((me // (1 << bit)) % 2))
    return me


def code_parts(code):
    high = jnp.floor(code * (1.0 / 256.0) + 0.5)
    return jnp.concatenate([high, code - 256.0 * high], axis=1).astype(bf16)


def from_parts(both):
    half = both.shape[1] // 2
    return 256.0 * both[:, :half] + both[:, half:]


def value_parts(x):
    high = x.astype(bf16)
    return jnp.concatenate([high, (x - high.astype(f32)).astype(bf16)], axis=1)


def add_parts(both):
    half = both.shape[1] // 2
    return both[:, :half] + both[:, half:]


def pick(x, chunk):
    n = x.shape[1]
    if chunk == 0:
        return jnp.concatenate([x[:, 3 * n // 4 :], x[:, : n // 4]], axis=1)
    return x[:, n // 4 : 3 * n // 4]


def unpick(edge, middle):
    half = edge.shape[1] // 2
    return jnp.concatenate([edge[:, half:], middle, edge[:, :half]], axis=1)


def smooth(edge, middle, other):
    width = edge.shape[1]
    x = jnp.concatenate([edge, middle], axis=1)
    low = pltpu.roll(x, 1, 1)
    high = pltpu.roll(x, 2 * width - 1, 1)
    lane = lax.broadcasted_iota(i32, edge.shape, 1)
    low_edge = jnp.where(lane == width // 2, pltpu.roll(other, 1, 1), low[:, :width])
    high_edge = jnp.where(lane == width // 2 - 1, pltpu.roll(other, width - 1, 1), high[:, :width])
    new_edge = edge + span_mix * (high_edge - 2.0 * edge + low_edge)
    new_middle = middle + span_mix * (high[:, width:] - 2.0 * middle + low[:, width:])
    return unpick(new_edge, new_middle)


def kernel(
    fluids, metals, cap,
    valid_in, fluid_in, wall_in, cond_in, owner_in, slot_in, resp_in, cool_in, old_in,
    favg_out, mwall_out, wnew_out,
    favg_v, mwall_v, wnew_v, face_v, halo_f, wall_v, valid,
    cond, owner, slot, cool, fluid_v, resp_v, old_v,
    pack, unpack, spread, fetch,
    meta_s, meta_r, flux_s, flux_r,
    low_v, temp_v, halo_t, back_s, back_r, blevel_s, blevel_r,
    local_sem, meta_sem, flux_sem, low_sem, halo_sem, back_sem, blevel_sem,
):
    blocks, layers, cells, span_dev = fluid_v.shape
    rows = blocks * cells
    slots = resp_v.shape[0]
    width = span_dev // 2
    me_f, me_m, me_s = lax.axis_index("fluid"), lax.axis_index("metal"), lax.axis_index("span")
    peers = [partner(me_f, r) for r in range(fluids)]
    order = list(range(2, fluids)) + [1]
    across = [None] + [lax.rem(me_m + r, metals) for r in range(1, metals)]
    mate = 1 - me_s

    loads = [
        pltpu.make_async_copy(src, dst, local_sem.at[i])
        for i, (src, dst) in enumerate(
            (
                (valid_in, valid), (owner_in, owner), (slot_in, slot), (cond_in, cond),
                (wall_in, wall_v), (cool_in, cool), (old_in, old_v), (resp_in, resp_v),
            )
        )
    ]
    fluid_loads = [
        pltpu.make_async_copy(fluid_in.at[b], fluid_v.at[b], local_sem.at[11 + blocks + b])
        for b in range(blocks)
    ]
    for load in loads[:4] + fluid_loads + loads[4:5]:
        load.start()

    barrier = pltpu.get_barrier_semaphore()
    for r in order:
        pl.semaphore_signal(barrier, inc=1, device_id={"fluid": peers[r]}, device_id_type=MESH)
    for r in range(1, metals):
        pl.semaphore_signal(barrier, inc=1, device_id={"metal": across[r]}, device_id_type=MESH)
    pl.semaphore_signal(barrier, inc=1, device_id={"span": mate}, device_id_type=MESH)

    def remote(src, dst, sems, place, where):
        return pltpu.make_async_remote_copy(
            src_ref=src, dst_ref=dst, send_sem=sems.at[(0, *place)], recv_sem=sems.at[(1, *place)],
            device_id=where, device_id_type=MESH,
        )

    for load in loads[:3]:
        load.wait()

    away = jnp.concatenate([owner[b : b + 1, :] for b in range(blocks)], axis=1) ^ me_f
    cell = lax.broadcasted_iota(i32, (1, cells), 1)
    live = jnp.concatenate([(cell < valid[0:1, b : b + 1]).astype(i32) for b in range(blocks)], axis=1)
    away = jnp.where(live > 0, away, -1)
    lines = -(-fluids // 16) * 16
    chosen = lax.broadcasted_iota(i32, (lines, rows), 0) == away
    before = lax.broadcasted_iota(i32, (rows, rows), 0) < lax.broadcasted_iota(i32, (rows, rows), 1)
    earlier = mm(chosen.astype(f32).astype(bf16), before.astype(f32).astype(bf16))
    ordinal = jnp.sum(jnp.where(chosen, earlier, 0.0), axis=0, keepdims=True)
    place = jnp.where(away >= 0, away.astype(f32) * cap + ordinal, -1.0)
    total = fluids * cap
    pack[...] = (
        lax.broadcasted_iota(i32, (total, rows), 0).astype(f32) == place
    ).astype(f32).astype(bf16)
    slot_row = jnp.concatenate([slot[b : b + 1, :] for b in range(blocks)], axis=1)
    line = lax.broadcasted_iota(i32, (16, rows), 0)
    halves = jnp.where(line == 0, slot_row // 256, jnp.where(line == 1, slot_row % 256, 0))
    packed_slots = lax.dot_general(
        halves.astype(f32).astype(bf16), pack[...], (((1,), (1,)), ((), ())),
        preferred_element_type=f32,
    )
    packed_slots = 256.0 * packed_slots[0:1] + packed_slots[1:2]
    for load in loads[3:5]:
        load.wait()
    weights = [2.0 * (layers - l) / (layers * (layers + 1.0)) for l in range(layers)]
    flux = []
    for b in range(blocks):
        fluid_loads[b].wait()
        near = weights[0] * fluid_v[b, 0].astype(f32)
        for l in range(1, layers):
            near = near + weights[l] * fluid_v[b, l].astype(f32)
        gain = to_column(cond[b : b + 1, :])
        lives = lax.broadcasted_iota(i32, (cells, 1), 0) < valid[0:1, b : b + 1]
        flux.append(
            jnp.where(lives, gain * (near - wall_v[b * cells : (b + 1) * cells, :]), 0.0)
        )
    flux = jnp.concatenate(flux, axis=0)
    for load in loads[5:]:
        load.start()

    flux, level = encode(flux)
    lanes = meta_s.shape[2] - width
    for r in range(fluids):
        meta_s[r, :, 0:cap] = packed_slots[:, r * cap : (r + 1) * cap]
        meta_s[r, :, lanes:] = jnp.broadcast_to(level, (1, width))

    pl.semaphore_wait(barrier, fluids + metals - 1)
    sends = []

    def send(copy):
        copy.start()
        sends.append(copy)
        return copy

    metas = [
        send(remote(meta_s.at[r], meta_r.at[r], meta_sem, (r,), {"fluid": peers[r]}))
        for r in order
    ]

    fluxes = []
    for c in range(2):
        fill(flux_r, flux_s, c, from_parts(mm(pack[...], code_parts(pick(flux, c)))), cap)
        fluxes.append(
            [
                send(remote(flux_s.at[c, r], flux_r.at[c, r], flux_sem, (c, r), {"fluid": peers[r]}))
                for r in order
            ]
        )
    unpack[...] = (
        lax.broadcasted_iota(i32, (rows, total), 1).astype(f32) == to_column(place)
    ).astype(f32).astype(bf16)

    for copy in metas:
        copy.wait_recv()
    arrived = jnp.concatenate(
        [packed_slots[:, 0:cap]] + [meta_r[r, :, 0:cap] for r in range(1, fluids)], axis=1
    )
    spread[...] = (
        lax.broadcasted_iota(i32, (slots, total), 0).astype(f32) == arrived
    ).astype(f32).astype(bf16)
    fetch[...] = (
        lax.broadcasted_iota(i32, (total, slots), 1).astype(f32) == to_column(arrived)
    ).astype(f32).astype(bf16)
    for load in loads[5:]:
        load.wait()
    cool_col = to_column(cool[...])

    averages, lows, backs = [], [], []
    for c in range(2):
        for copy in fluxes[c]:
            copy.wait_recv()
        incoming = jnp.concatenate(
            [
                decode(flux_r[c, r], (meta_r if r else meta_s)[r, :, lanes:])
                for r in range(fluids)
            ], axis=0
        )
        summed = add_parts(mm(spread[...], value_parts(incoming)))
        average = (1.0 - average_weight) * pick(old_v[...], c) + average_weight * summed
        averages.append(average)
        low_v[c, 0] = average.astype(bf16)
        lows.append(
            [
                send(remote(low_v.at[c, 0], low_v.at[c, r], low_sem, (c, r), {"metal": across[r]}))
                for r in range(1, metals)
            ]
        )
    for c in range(2):
        temp = cool_col
        for r in range(metals):
            if r:
                lows[c][r - 1].wait_recv()
            stripe = lax.rem(me_m + metals - r, metals)
            columns = pl.ds(pl.multiple_of(stripe * slots, slots), slots)
            temp = temp + mm(resp_v[:, columns], low_v[c, r])
        temp_v[c] = temp
        if c == 0:
            edge_t = send(remote(temp_v.at[0], halo_t, halo_sem, (0,), {"span": mate}))
        code, level = encode(temp)
        blevel_s[c] = jnp.broadcast_to(level, (1, width))
        fill(back_r, back_s, c, from_parts(mm(fetch[...], code_parts(code))), cap)
        backs.append(
            [
                send(remote(blevel_s.at[c], blevel_r.at[c, r], blevel_sem, (c, r), {"fluid": peers[r]}))
                for r in order
            ]
            + [
                send(remote(back_s.at[c, r], back_r.at[c, r], back_sem, (c, r), {"fluid": peers[r]}))
                for r in order
            ]
        )

    favg_v[...] = unpick(*averages)
    stores = [pltpu.make_async_copy(favg_v, favg_out, local_sem.at[9])]
    stores[0].start()
    edge_t.wait_recv()
    mwall_v[...] = smooth(temp_v[0], temp_v[1], halo_t[...])
    stores.append(pltpu.make_async_copy(mwall_v, mwall_out, local_sem.at[10]))
    stores[1].start()

    for c in range(2):
        for copy in backs[c]:
            copy.wait_recv()
        returned = jnp.concatenate(
            [
                decode(back_r[c, r], blevel_r[c, r] if r else blevel_s[c])
                for r in range(fluids)
            ], axis=0
        )
        face_v[c] = add_parts(mm(unpack[...], value_parts(returned)))
        if c == 0:
            edge_f = send(remote(face_v.at[0], halo_f, halo_sem, (1,), {"span": mate}))
    edge_f.wait_recv()
    for b in range(blocks):
        lives = lax.broadcasted_iota(i32, (cells, 1), 0) < valid[0:1, b : b + 1]
        part = pl.ds(b * cells, cells)
        face = smooth(face_v[0, part, :], face_v[1, part, :], halo_f[part, :])
        wnew_v[part, :] = jnp.where(
            lives, (1.0 - relaxation) * wall_v[part, :] + relaxation * face, 0.0
        )
        store = pltpu.make_async_copy(
            wnew_v.at[part, :], wnew_out.at[part, :], local_sem.at[11 + b]
        )
        store.start()
        stores.append(store)
    for copy in sends:
        copy.wait_send()
    for store in stores:
        store.wait()


def hand_over(*refs):
    count = (len(refs) - 2) // 3
    sources, targets, held, (load_sem, store_sem) = (
        refs[:count], refs[count : 2 * count], refs[2 * count : 3 * count], refs[3 * count :]
    )
    loads = [pltpu.make_async_copy(sources[i], held[i], load_sem.at[i]) for i in range(count)]
    stores = [pltpu.make_async_copy(held[i], targets[i], store_sem.at[i]) for i in range(count)]
    for load in loads:
        load.start()
    for load, store in zip(loads, stores):
        load.wait()
        store.start()
    for store in stores:
        store.wait()


def body(
    fluid_temp, wall_old, conductance, valid_rows, face_owner, face_slot, response, coolant, flux_old
):
    blocks, layers, cells, span_dev = fluid_temp.shape
    rows = blocks * cells
    fluids, metals = lax.axis_size("fluid"), lax.axis_size("metal")
    cap = -(-(3 * rows // (2 * fluids)) // 16) * 16
    lanes = -(-cap // 128) * 128
    slots = response.shape[1]
    width = span_dev // 2
    total = fluids * cap
    hbm = pl.BlockSpec(memory_space=pltpu.HBM)
    dma = pltpu.SemaphoreType.DMA
    held = pl.pallas_call(
        functools.partial(kernel, fluids, metals, cap),
        out_shape=[
            jax.ShapeDtypeStruct((slots, span_dev), f32),
            jax.ShapeDtypeStruct((slots, span_dev), f32),
            jax.ShapeDtypeStruct((rows, span_dev), f32),
        ],
        in_specs=[hbm] * 9,
        out_specs=[hbm] * 3,
        scratch_shapes=[
            pltpu.VMEM((slots, span_dev), f32),
            pltpu.VMEM((slots, span_dev), f32),
            pltpu.VMEM((rows, span_dev), f32),
            pltpu.VMEM((2, rows, width), f32),
            pltpu.VMEM((rows, width), f32),
            pltpu.VMEM((rows, span_dev), f32),
            pltpu.VMEM((1, blocks), i32),
            pltpu.VMEM((blocks, cells), f32),
            pltpu.VMEM((blocks, cells), i32),
            pltpu.VMEM((blocks, cells), i32),
            pltpu.VMEM((1, slots), f32),
            pltpu.VMEM(fluid_temp.shape, bf16),
            pltpu.VMEM(response.shape[1:], bf16),
            pltpu.VMEM((slots, span_dev), f32),
            pltpu.VMEM((total, rows), bf16),
            pltpu.VMEM((rows, total), bf16),
            pltpu.VMEM((slots, total), bf16),
            pltpu.VMEM((total, slots), bf16),
            pltpu.VMEM((fluids, 1, lanes + width), f32),
            pltpu.VMEM((fluids, 1, lanes + width), f32),
            pltpu.VMEM((2, fluids, cap, width), i16),
            pltpu.VMEM((2, fluids, cap, width), i16),
            pltpu.VMEM((2, metals, slots, width), bf16),
            pltpu.VMEM((2, slots, width), f32),
            pltpu.VMEM((slots, width), f32),
            pltpu.VMEM((2, fluids, cap, width), i16),
            pltpu.VMEM((2, fluids, cap, width), i16),
            pltpu.VMEM((2, 1, width), f32),
            pltpu.VMEM((2, fluids, 1, width), f32),
            dma((11 + 2 * blocks,)),
            dma((2, fluids)),
            dma((2, 2, fluids)),
            dma((2, 2, metals)),
            dma((2, 2)),
            dma((2, 2, fluids)),
            dma((2, 2, fluids)),
        ],
        compiler_params=pltpu.CompilerParams(
            collective_id=0, has_side_effects=True, vmem_limit_bytes=vmem_grant
        ),
    )(
        valid_rows.reshape(1, blocks),
        fluid_temp,
        wall_old.reshape(rows, span_dev),
        conductance,
        face_owner.reshape(blocks, cells),
        face_slot,
        response[0],
        coolant,
        flux_old[0],
    )
    out = pl.pallas_call(
        hand_over,
        out_shape=[jax.ShapeDtypeStruct(x.shape, x.dtype) for x in held],
        in_specs=[hbm] * 3,
        out_specs=[hbm] * 3,
        scratch_shapes=[pltpu.VMEM(x.shape, x.dtype) for x in held] + [dma((3,)), dma((3,))],
        compiler_params=pltpu.CompilerParams(vmem_limit_bytes=vmem_grant),
    )(*held)
    return out[0][None], out[1][None], out[2].reshape(blocks, cells, span_dev)


def solution(mesh):
    in_specs = (
        P(("groups", "fluid", "metal"), None, None, "span"),
        P(("groups", "fluid", "metal"), None, "span"),
        P(("groups", "fluid", "metal"), None),
        P(("groups", "fluid", "metal")),
        P(("groups", "fluid", "metal"), None, None),
        P(("groups", "fluid", "metal"), None),
        P("fluid", "metal", None),
        P("fluid", "metal"),
        P(("groups", "fluid"), "metal", "span"),
    )
    out_specs = (
        P(("groups", "fluid"), "metal", "span"),
        P(("groups", "fluid"), "metal", "span"),
        P(("groups", "fluid", "metal"), None, "span"),
    )
    return jax.shard_map(body, mesh=mesh, in_specs=in_specs, out_specs=out_specs, check_vma=False)
```
